512 devices in a mesh: rows: 128 (over z_hi, x, y), feat: 4 (over z_lo, core).
Axes of the slice: x: 4, y: 8, z: 8 (z_hi: 4, z_lo: 2; z = z_hi * 2 + z_lo), core: 2. Of those that a mesh axis runs over, the one named last changes fastest.
Arguments:
- bin_ids: int32 [128, 262144], P('feat', 'rows'), may hold values from 0 to 255
- node_ids: int32 [262144], P('rows'), may hold values from 0 to 31, as said below
- gradients: bfloat16 [262144], P('rows'), may hold values from -6 to 6
- hessians: bfloat16 [262144], P('rows'), may hold values from 0.099609375 to 1
Outputs:
- gain_table: float32 [128, 32, 256], P('feat')
- best_gain: float32 [32], replicated
The draws below stay inside these ranges and needn't reach their ends.
Inputs may be any that keep to these rules, and one draw needn't show every extreme that they name: `node_ids`: on some device all 2048 rows lie in one node; on other devices anywhere from none to all rows may lie in one node, and node sizes are very uneven.
All inputs are finite; a program needn't handle non-finite values.
Results may differ from the reference program's by a relative error of at most 0.0003.
Values sent between devices are 32-bit elements; how exact they have to be, the bound alone decides.
A program may use at most 64 MiB of HBM per device.

```python
import math
import jax
import jax.numpy as jnp
from jax import lax

F = 128
BINS = 256
NODES = 32
ROWS_DEV = 2048
NROWS = 262144


def draw_node_ids(key, part):
    key = jax.random.fold_in(key, 11)
    subkeys = jax.random.split(key, 7)
    device_count = NROWS // ROWS_DEV
    ranking = jax.random.permutation(subkeys[0], NODES)
    draw_one = jax.random.randint(subkeys[1], (NROWS,), 0, NODES)
    draw_two = jax.random.randint(subkeys[2], (NROWS,), 0, NODES)
    background = ranking[jnp.minimum(draw_one, draw_two)]
    dominant = jax.random.randint(subkeys[3], (device_count,), 0, NODES)
    portion = jax.random.randint(subkeys[4], (device_count,), 0, 1001)
    chosen = jax.random.randint(subkeys[5], (), 0, device_count)
    portion = jnp.where(jnp.arange(device_count) == chosen, 1000, portion)
    toss_draw = jax.random.randint(subkeys[6], (NROWS,), 0, 1000)
    device = jnp.arange(NROWS) // ROWS_DEV
    return jnp.where(toss_draw < portion[device], dominant[device], background).astype(jnp.int32)


def draw_bin_ids(key, part):
    key = jax.random.fold_in(key, 23)
    subkeys = jax.random.split(key, 4)
    flavour = jax.random.randint(subkeys[0], (F, 1), 0, 4)
    evenly = jax.random.randint(subkeys[1], (F, NROWS), 0, BINS)
    partner = jax.random.randint(subkeys[2], (F, NROWS), 0, BINS)
    toss_draw = jax.random.randint(subkeys[3], (F, NROWS), 0, 10)
    sparse = jnp.where(toss_draw < 7, 0, evenly)
    lowered = jnp.minimum(evenly, partner)
    mixed = jnp.where(flavour == 0, sparse, jnp.where(flavour == 1, lowered, evenly))
    return mixed.astype(jnp.int32)


def levels(stream_key, extent, pieces, low, high):
    loudness = 1.0
    for position, shards_of in pieces:
        draws = jax.random.uniform(jax.random.fold_in(jax.random.fold_in(stream_key, 6), position), (shards_of,), jnp.float32, low / len(pieces), high / len(pieces))
        loudness = loudness * jnp.repeat(jnp.exp(draws), extent[position] // shards_of).reshape((-1,) + (1,) * (len(extent) - 1 - position))
    return loudness


def normal_values(own_key, extent, deviation, bound, shards=(), dtype=jnp.bfloat16):
    factor_of = levels(own_key, extent, shards, -0.22, 0.18) if shards else 1.0
    drawn = jax.random.normal(own_key, extent, jnp.float32) * deviation * factor_of
    return jnp.minimum(jnp.maximum(drawn, -bound), bound).astype(dtype)


def setup_inputs(seed: int = 0) -> dict:
    splits = jax.random.split(jax.random.key(seed), 5)
    return {
        "bin_ids": draw_bin_ids(jax.random.fold_in(splits[4], 71), 0),
        "node_ids": draw_node_ids(jax.random.fold_in(splits[4], 71), 0),
        "gradients": normal_values(splits[2], (NROWS,), 1.0, 6.0, ((0, 128),)),
        "hessians": jnp.clip(jnp.exp(math.log(1.0) - 2.306499 * jax.random.uniform(splits[3], (NROWS,), jnp.float32) ** levels(splits[3], (NROWS,), ((0, 128),), -0.2, 0.2)), 0.099609375, 1.0).astype(jnp.bfloat16),
    }


def gains_of(grad_hist, hess_hist):
    left_grad = jnp.cumsum(grad_hist, axis=-1)
    left_hess = jnp.cumsum(hess_hist, axis=-1)
    total_grad = jnp.sum(grad_hist, axis=-1, keepdims=True)
    total_hess = jnp.sum(hess_hist, axis=-1, keepdims=True)
    lam = jnp.float32(1.0)
    right_grad = total_grad - left_grad
    right_hess = total_hess - left_hess
    return (left_grad * left_grad / (left_hess + lam) + right_grad * right_grad / (right_hess + lam)
            - total_grad * total_grad / (total_hess + lam))


def reference(bin_ids, node_ids, gradients, hessians):
    grad_f = gradients.astype(jnp.float32)
    hess_f = hessians.astype(jnp.float32)

    def one_feature(column):
        slots = (node_ids * BINS + column).astype(jnp.int32)
        grad_hist = jax.ops.segment_sum(grad_f, slots, num_segments=NODES * BINS)
        hess_hist = jax.ops.segment_sum(hess_f, slots, num_segments=NODES * BINS)
        return gains_of(grad_hist.reshape(NODES, BINS), hess_hist.reshape(NODES, BINS))

    gain_table = lax.map(one_feature, bin_ids)
    best_gain = jnp.max(gain_table, axis=(0, 2))
    return gain_table, best_gain
```

```python
import functools

import jax
import jax.numpy as jnp
from jax import lax
from jax.experimental import pallas as pl
from jax.experimental.pallas import tpu as pltpu
from jax.sharding import PartitionSpec as P

MESH = pl.DeviceIdType.MESH
BINS = 256
NODES = 32
HALF = 128
NX, NY, NZ = 4, 8, 4
NF = 8
ROWS = 2048
CH = 2 * NODES
QUARTER = 2 * NODES // NZ


def build_weights(aux, weights, slot):
    row = lax.broadcasted_iota(jnp.int32, (CH, HALF), 0)
    node_of = ((row // QUARTER) * 8 + row % 8).astype(jnp.float32)
    is_grad = (row % QUARTER) < 8
    for i in range(ROWS // HALF):
        node = jnp.broadcast_to(aux[slot, 0, i : i + 1, :], (CH, HALF))
        grad = jnp.broadcast_to(aux[slot, 1, i : i + 1, :], (CH, HALF))
        hess = jnp.broadcast_to(aux[slot, 2, i : i + 1, :], (CH, HALF))
        value = jnp.where(node == node_of, jnp.where(is_grad, grad, hess), 0.0)
        weights[slot, :, i * HALF : (i + 1) * HALF] = value.astype(jnp.bfloat16)


def partial_hist(bins, weights, levels, slot, feature):
    ids = bins[slot, pl.ds(feature, 1), :]
    high = jnp.broadcast_to(ids >= HALF, (CH, ROWS))
    low = (ids & (HALF - 1)).astype(jnp.float32).astype(jnp.bfloat16)
    w = weights[slot]
    zero = jnp.zeros_like(w)
    left = jnp.concatenate([jnp.where(high, zero, w), jnp.where(high, w, zero)], axis=0)
    hot = jnp.where(jnp.broadcast_to(low, (HALF, ROWS)) == levels, jnp.bfloat16(1), jnp.bfloat16(0))
    return lax.dot_general(left, hot, (((1,), (1,)), ((), ())), preferred_element_type=jnp.float32)


def side_by_side(d):
    return jnp.concatenate([d[:CH], d[CH:]], axis=1)


def prefix_sums(values):
    r = lax.broadcasted_iota(jnp.int32, (BINS, BINS), 0)
    c = lax.broadcasted_iota(jnp.int32, (BINS, BINS), 1)
    upto = jnp.where(r <= c, 1.0, 0.0).astype(jnp.bfloat16)
    first = values.astype(jnp.bfloat16)
    rest = values - first.astype(jnp.float32)
    second = rest.astype(jnp.bfloat16)
    third = (rest - second.astype(jnp.float32)).astype(jnp.bfloat16)
    n = values.shape[0]
    parts = jnp.concatenate([first.astype(jnp.float32), second.astype(jnp.float32), third.astype(jnp.float32)], axis=0)
    sums = jnp.dot(parts.astype(jnp.bfloat16), upto, preferred_element_type=jnp.float32)
    left = (sums[2 * n :] + sums[n : 2 * n]) + sums[:n]
    total = jnp.broadcast_to(left[:, BINS - 1 :], left.shape)
    return left, total


def kernel(bins_hbm, aux_hbm, table, best,
           bins, aux, weights, acc, inbox_y, mine, inbox_z, tops,
           local_sems, a_send, a_recv, w_send, w_recv, y_send, y_recv, z_send, z_recv,
           gz_send, gz_recv, gy_send, gy_recv, gx_send, gx_recv, f_send, f_recv, ready):
    r = lax.axis_index("rows")
    f = lax.axis_index("feat")
    zh, x, y = r // (NX * NY), (r // NY) % NX, r % NY
    zl, core = f // 2, f % 2

    def at(dz, dx, dy, dzl=0, dc=0):
        row = (((zh + dz) % NZ) * NX + (x + dx) % NX) * NY + (y + dy) % NY
        return (row, ((zl + dzl) % 2) * 2 + (core + dc) % 2)

    def remote(src, dst, send, recv, to):
        return pltpu.make_async_remote_copy(src_ref=src, dst_ref=dst, send_sem=send, recv_sem=recv, device_id=to, device_id_type=MESH)

    barrier = pltpu.get_barrier_semaphore()
    near = [at(0, 1, 0), at(0, 2, 0), at(0, 3, 0), at(0, 0, 1), at(0, 0, 2), at(0, 0, 6), at(0, 0, 7),
            at(1, 0, 0), at(3, 0, 0), at(0, 0, 0, 1, 0), at(0, 0, 0, 0, 1), at(0, 0, 0, 1, 1)]
    for to in near:
        pl.semaphore_signal(barrier, inc=1, device_id=to, device_id_type=MESH)

    own_bins = pltpu.make_async_copy(bins_hbm.at[pl.ds(pl.multiple_of(x * NF, NF), NF)], bins.at[0], local_sems.at[0])
    own_aux = pltpu.make_async_copy(aux_hbm, aux.at[0], local_sems.at[1])
    own_bins.start()
    own_aux.start()
    pl.semaphore_wait(barrier, len(near))

    exchange = []
    for d in (2, 1, 3):
        to = at(0, d, 0)
        start = pl.multiple_of(((x + d) % NX) * NF, NF)
        exchange.append(remote(aux_hbm, aux.at[d], w_send.at[d], w_recv.at[d], to))
        exchange.append(remote(bins_hbm.at[pl.ds(start, NF)], bins.at[d], a_send.at[d], a_recv.at[d], to))
    for copy in exchange:
        copy.start()
    for to in (at(0, 0, 2), at(0, 0, 6), at(1, 0, 0), at(3, 0, 0)):
        pl.semaphore_signal(ready, inc=1, device_id=to, device_id_type=MESH)

    levels = lax.broadcasted_iota(jnp.int32, (HALF, ROWS), 0).astype(jnp.float32).astype(jnp.bfloat16)
    own_aux.wait()
    own_bins.wait()
    build_weights(aux, weights, 0)

    @pl.loop(0, NF, unroll=4)
    def _(j):
        acc[j] = side_by_side(partial_hist(bins, weights, levels, 0, j))

    for copy in exchange:
        copy.wait()
    for s in (1, 3, 2):
        build_weights(aux, weights, s)
    pl.semaphore_wait(ready, 4)

    @pl.loop(0, NF, unroll=2)
    def _(i):
        m = (i + 1) // 2
        k = (NY // 2 + m * (1 - 2 * (i % 2))) % NY
        j = (y + k) % NY
        d = partial_hist(bins, weights, levels, 1, j)
        d += partial_hist(bins, weights, levels, 3, j)
        d += partial_hist(bins, weights, levels, 2, j)
        acc[j] = acc[j] + side_by_side(d)

        @pl.when(i < NF - 1)
        def _():
            remote(acc.at[j], inbox_y.at[k], y_send.at[k], y_recv.at[k], at(0, 0, k)).start()

    total = acc[y]
    for k in (4, 3, 5, 2, 6, 1, 7):
        copy = remote(acc.at[0], inbox_y.at[k], y_send.at[k], y_recv.at[k], at(0, 0, k))
        copy.wait_recv()
        total = total + inbox_y[k]
    mine[...] = total

    copies = []
    for d in (2, 1, 3):
        q = (zh + d) % NZ
        copy = remote(mine.at[pl.ds(pl.multiple_of(q * QUARTER, QUARTER), QUARTER)], inbox_z.at[d], z_send.at[d], z_recv.at[d], at(d, 0, 0))
        copy.start()
        copies.append(copy)
    hist = mine[pl.ds(pl.multiple_of(zh * QUARTER, QUARTER), QUARTER), :]
    for copy, d in zip(copies, (2, 1, 3)):
        copy.wait_recv()
        hist = hist + inbox_z[d]

    left, whole = prefix_sums(hist)
    lg, lh, tg, th = left[:8], left[8:], whole[:8], whole[8:]
    rg, rh = tg - lg, th - lh
    gains = lg * lg / (lh + 1.0) + rg * rg / (rh + 1.0) - tg * tg / (th + 1.0)

    me = x * NF + y
    rows = pl.ds(pl.multiple_of(zh * 8, 8), 8)
    table[me, rows, :] = gains

    gathers = []
    for d in (2, 1, 3):
        copy = remote(table.at[me, rows], table.at[me, rows], gz_send.at[d], gz_recv.at[d], at(d, 0, 0))
        copy.start()
        gathers.append(copy)
    for copy in gathers:
        copy.wait_recv()

    sent = list(gathers)
    arrive = {}
    for k in (4, 3, 5, 2, 6, 1, 7):
        copy = remote(table.at[me], table.at[me], gy_send.at[k], gy_recv.at[k], at(0, 0, k))
        copy.start()
        sent.append(copy)
        arrive[k] = copy
    last = []
    for k in (0, 1, 7, 2, 6, 3, 5, 4):
        if k:
            arrive[k].wait_recv()
        here = x * NF + (y + NY - k) % NY
        for d in (2, 1, 3):
            copy = remote(table.at[here], table.at[here], gx_send.at[d, k], gx_recv.at[d, k], at(0, d, 0))
            copy.start()
            sent.append(copy)
            last.append(copy)
    for copy in last:
        copy.wait_recv()

    top = jnp.max(table[...], axis=0)
    tops[0] = jnp.broadcast_to(jnp.max(top, axis=1, keepdims=True), (NODES, HALF))
    fins = []
    for n, (dzl, dc) in enumerate(((1, 0), (0, 1), (1, 1)), 1):
        copy = remote(tops.at[0], tops.at[n], f_send.at[n], f_recv.at[n], at(0, 0, 0, dzl, dc))
        copy.start()
        fins.append(copy)
    for copy in sent:
        copy.wait_send()
    for copy in copies:
        copy.wait_send()
    for k in range(1, NY):
        remote(acc.at[0], inbox_y.at[k], y_send.at[k], y_recv.at[k], at(0, 0, k)).wait_send()
    for copy in fins:
        copy.wait()
    over = jnp.maximum(jnp.maximum(tops[0], tops[1]), jnp.maximum(tops[2], tops[3]))
    lane = lax.broadcasted_iota(jnp.int32, (NODES, HALF), 1)
    node = lax.broadcasted_iota(jnp.int32, (NODES, HALF), 0)
    best[...] = jnp.max(jnp.where(lane == node, over, -jnp.inf), axis=0, keepdims=True)


def per_device(bin_ids, node_ids, gradients, hessians):
    f32 = jnp.float32
    aux = jnp.stack([node_ids.astype(f32), gradients.astype(f32), hessians.astype(f32)]).reshape(3, ROWS // HALF, HALF)
    dma = pltpu.SemaphoreType.DMA
    table, best = pl.pallas_call(
        kernel,
        out_shape=(
            jax.ShapeDtypeStruct((NX * NF, NODES, BINS), f32),
            jax.ShapeDtypeStruct((1, HALF), f32),
        ),
        in_specs=[pl.BlockSpec(memory_space=pl.ANY)] * 2,
        out_specs=(pl.BlockSpec(memory_space=pltpu.VMEM), pl.BlockSpec(memory_space=pltpu.VMEM)),
        scratch_shapes=[
            pltpu.VMEM((NX, NF, ROWS), jnp.int32),
            pltpu.VMEM((NX, 3, ROWS // HALF, HALF), f32),
            pltpu.VMEM((NX, CH, ROWS), jnp.bfloat16),
            pltpu.VMEM((NF, CH, BINS), f32),
            pltpu.VMEM((NY, CH, BINS), f32),
            pltpu.VMEM((CH, BINS), f32),
            pltpu.VMEM((NZ, QUARTER, BINS), f32),
            pltpu.VMEM((4, NODES, HALF), f32),
            dma((2,)),
            dma((NX,)), dma((NX,)),
            dma((NX,)), dma((NX,)),
            dma((NY,)), dma((NY,)),
            dma((NZ,)), dma((NZ,)),
            dma((NZ,)), dma((NZ,)),
            dma((NY,)), dma((NY,)),
            dma((NX, NY)), dma((NX, NY)),
            dma((4,)), dma((4,)),
            pltpu.SemaphoreType.REGULAR,
        ],
        compiler_params=pltpu.CompilerParams(collective_id=0, has_side_effects=True, vmem_limit_bytes=40 * 2**20),
        cost_estimate=pl.CostEstimate(flops=2 * 32 * ROWS * CH * BINS, bytes_accessed=2 * 2**20, transcendentals=0),
        name="split_gains",
    )(bin_ids, aux)
    return table, best[0, :NODES]


def solution(mesh):
    in_specs = (P("feat", "rows"), P("rows"), P("rows"), P("rows"))
    out_specs = (P("feat", None, None), P())
    return jax.shard_map(per_device, mesh=mesh, in_specs=in_specs, out_specs=out_specs, check_vma=False)
```

```python
import functools

import jax
import jax.numpy as jnp
from jax import lax
from jax.experimental import pallas as pl
from jax.experimental.pallas import tpu as pltpu
from jax.sharding import PartitionSpec as P

MESH = pl.DeviceIdType.MESH
BINS = 256
NODES = 32
HALF = 128
NX, NY, NZ = 4, 8, 4
NG = 4
ROWS = 2048
CH = 2 * NODES
QUARTER = 2 * NODES // NZ


def build_weights(aux, weights, slot):
    row = lax.broadcasted_iota(jnp.int32, (CH, HALF), 0)
    node_of = ((row // QUARTER) * 8 + row % 8).astype(jnp.float32)
    is_grad = (row % QUARTER) < 8
    for i in range(ROWS // HALF):
        node = jnp.broadcast_to(aux[slot, 0, i : i + 1, :], (CH, HALF))
        grad = jnp.broadcast_to(aux[slot, 1, i : i + 1, :], (CH, HALF))
        hess = jnp.broadcast_to(aux[slot, 2, i : i + 1, :], (CH, HALF))
        value = jnp.where(node == node_of, jnp.where(is_grad, grad, hess), 0.0)
        weights[slot, :, i * HALF : (i + 1) * HALF] = value.astype(jnp.bfloat16)


def partial_hist(bins, weights, levels, slot, feature):
    ids = bins[slot, pl.ds(feature, 1), :]
    high = jnp.broadcast_to(ids >= HALF, (CH, ROWS))
    low = (ids & (HALF - 1)).astype(jnp.float32).astype(jnp.bfloat16)
    w = weights[slot]
    zero = jnp.zeros_like(w)
    left = jnp.concatenate([jnp.where(high, zero, w), jnp.where(high, w, zero)], axis=0)
    hot = jnp.where(jnp.broadcast_to(low, (HALF, ROWS)) == levels, jnp.bfloat16(1), jnp.bfloat16(0))
    return lax.dot_general(left, hot, (((1,), (1,)), ((), ())), preferred_element_type=jnp.float32)


def side_by_side(d):
    return jnp.concatenate([d[:CH], d[CH:]], axis=1)


def prefix_sums(values):
    r = lax.broadcasted_iota(jnp.int32, (BINS, BINS), 0)
    c = lax.broadcasted_iota(jnp.int32, (BINS, BINS), 1)
    upto = jnp.where(r <= c, 1.0, 0.0).astype(jnp.bfloat16)
    first = values.astype(jnp.bfloat16)
    rest = values - first.astype(jnp.float32)
    second = rest.astype(jnp.bfloat16)
    third = (rest - second.astype(jnp.float32)).astype(jnp.bfloat16)
    n = values.shape[0]
    parts = jnp.concatenate([first.astype(jnp.float32), second.astype(jnp.float32), third.astype(jnp.float32)], axis=0)
    sums = jnp.dot(parts.astype(jnp.bfloat16), upto, preferred_element_type=jnp.float32)
    left = (sums[2 * n :] + sums[n : 2 * n]) + sums[:n]
    total = jnp.broadcast_to(left[:, BINS - 1 :], left.shape)
    return left, total


def kernel(bins_hbm, aux_hbm, table, best,
           bins, aux, weights, acc, inbox, tops,
           local_sems, a_send, a_recv, w_send, w_recv, h_send, h_recv,
           g_send, g_recv, x_send, x_recv, f_send, f_recv, ready):
    r = lax.axis_index("rows")
    f = lax.axis_index("feat")
    zh, x, y = r // (NX * NY), (r // NY) % NX, r % NY
    zl, core = f // 2, f % 2
    yh, yl = y // 2, y % 2

    def at(dz, dx, dy, dzl=0, dc=0):
        row = (((zh + dz) % NZ) * NX + (x + dx) % NX) * NY + (y + dy) % NY
        return (row, ((zl + dzl) % 2) * 2 + (core + dc) % 2)

    def pair(dx, p):
        return at(0, dx, (1 - 2 * yl) * p)

    def remote(src, dst, send, recv, to):
        return pltpu.make_async_remote_copy(src_ref=src, dst_ref=dst, send_sem=send, recv_sem=recv, device_id=to, device_id_type=MESH)

    barrier = pltpu.get_barrier_semaphore()
    near = [pair(2, 1), pair(1, 1), pair(3, 1), at(0, 2, 0), at(0, 1, 0), at(0, 3, 0),
            at(0, 0, 2), at(0, 0, 6), at(1, 0, 0), at(3, 0, 0), at(0, 0, 1), at(0, 0, 7),
            at(0, 0, 0, 1, 0), at(0, 0, 0, 0, 1), at(0, 0, 0, 1, 1)]
    for to in near:
        pl.semaphore_signal(barrier, inc=1, device_id=to, device_id_type=MESH)

    def features_of(dx, p):
        group = ((x + dx) % NX) * 2 + (yl + p) % 2
        return pl.ds(group * NG, NG)

    own_bins = pltpu.make_async_copy(bins_hbm.at[features_of(0, 0)], bins.at[0], local_sems.at[0])
    own_aux = pltpu.make_async_copy(aux_hbm, aux.at[0], local_sems.at[1])
    own_bins.start()
    own_aux.start()
    pl.semaphore_wait(barrier, len(near))

    exchange = {}
    for dx, p in ((1, 0), (3, 0), (0, 1), (2, 0), (1, 1), (3, 1), (2, 1)):
        s = dx * 2 + p
        to = pair(dx, p)
        exchange[s] = (
            remote(aux_hbm, aux.at[s], w_send.at[s], w_recv.at[s], to),
            remote(bins_hbm.at[features_of(dx, p)], bins.at[s], a_send.at[s], a_recv.at[s], to),
        )
        for copy in exchange[s]:
            copy.start()
    for to in (at(0, 0, 2), at(0, 0, 6), at(1, 0, 0), at(3, 0, 0)):
        pl.semaphore_signal(ready.at[0], inc=1, device_id=to, device_id_type=MESH)

    levels = lax.broadcasted_iota(jnp.int32, (HALF, ROWS), 0).astype(jnp.float32).astype(jnp.bfloat16)
    own_aux.wait()
    own_bins.wait()
    build_weights(aux, weights, 0)

    @pl.loop(0, NG, unroll=4)
    def _(j):
        acc[j] = side_by_side(partial_hist(bins, weights, levels, 0, j))

    pl.semaphore_wait(ready.at[0], 4)
    for d in (2, 1, 3):
        pl.semaphore_signal(ready.at[1], inc=1, device_id=at(d, 0, 0), device_id_type=MESH)

    for s in (2, 6, 1):
        for copy in exchange[s]:
            copy.wait()
        build_weights(aux, weights, s)

        @pl.loop(0, NG, unroll=4)
        def _(j):
            acc[j] = acc[j] + side_by_side(partial_hist(bins, weights, levels, s, j))

    for s in (4, 3, 7, 5):
        for copy in exchange[s]:
            copy.wait()
        build_weights(aux, weights, s)
    pl.semaphore_wait(ready.at[1], 3)

    @pl.loop(0, NG, unroll=2)
    def _(i):
        m = (i + 1) // 2
        a = (2 + m * (1 - 2 * (i % 2))) % 4
        j = (yh + a) % 4
        d = partial_hist(bins, weights, levels, 4, j)
        for s in (3, 7, 5):
            d += partial_hist(bins, weights, levels, s, j)
        acc[j] = acc[j] + side_by_side(d)
        for b in (2, 1, 3, 0):
            quarter = pl.ds(pl.multiple_of(((zh + b) % NZ) * QUARTER, QUARTER), QUARTER)

            @pl.when(a + b > 0)
            def _():
                remote(acc.at[j, quarter], inbox.at[a, b], h_send.at[a, b], h_recv.at[a, b], at(b, 0, 2 * a)).start()

    hist = acc[yh, pl.ds(pl.multiple_of(zh * QUARTER, QUARTER), QUARTER), :]
    others = [(a, b) for a in (0, 1, 3, 2) for b in (0, 1, 3, 2) if a or b]
    for a, b in others:
        remote(acc.at[0, pl.ds(0, QUARTER)], inbox.at[a, b], h_send.at[a, b], h_recv.at[a, b], at(b, 0, 2 * a)).wait_recv()
        hist = hist + inbox[a, b]

    left, whole = prefix_sums(hist)
    lg, lh, tg, th = left[:8], left[8:], whole[:8], whole[8:]
    rg, rh = tg - lg, th - lh
    gains = lg * lg / (lh + 1.0) + rg * rg / (rh + 1.0) - tg * tg / (th + 1.0)

    def feature_at(dy):
        there = (y + dy) % NY
        return (x * 2 + there % 2) * NG + there // 2

    me = feature_at(0)
    rows = pl.ds(pl.multiple_of(zh * 8, 8), 8)
    table[me, rows, :] = gains

    sent = []
    arrive = {}
    for dy in (0, 4, 3, 5, 2, 6, 1, 7):
        for dz in (2, 1, 3, 0):
            if dy or dz:
                copy = remote(table.at[me, rows], table.at[me, rows], g_send.at[dy, dz], g_recv.at[dy, dz], at(dz, 0, dy))
                copy.start()
                sent.append(copy)
                arrive[dy, dz] = copy
    last = []
    for dy in (0, 1, 7, 2, 6, 3, 5, 4):
        for dz in range(NZ):
            if dy or dz:
                arrive[dy, dz].wait_recv()
        here = feature_at(NY - dy)
        for dx in (2, 1, 3):
            copy = remote(table.at[here], table.at[here], x_send.at[dx, dy], x_recv.at[dx, dy], at(0, dx, 0))
            copy.start()
            sent.append(copy)
            last.append(copy)

    top = jnp.max(table[pl.ds(x * 8, 8)], axis=0)
    over = jnp.broadcast_to(jnp.max(top, axis=1, keepdims=True), (NODES, HALF))
    lane = lax.broadcasted_iota(jnp.int32, (NODES, HALF), 1)
    node = lax.broadcasted_iota(jnp.int32, (NODES, HALF), 0)
    over = jnp.max(jnp.where(lane == node, over, -jnp.inf), axis=0, keepdims=True)
    tops[0] = jnp.broadcast_to(over, (8, HALF))
    fins = []
    for n in range(1, 16):
        copy = remote(tops.at[0], tops.at[n], f_send.at[n], f_recv.at[n], at(0, n // 4, 0, (n // 2) % 2, n % 2))
        copy.start()
        fins.append(copy)

    for a, b in others:
        remote(acc.at[0, pl.ds(0, QUARTER)], inbox.at[a, b], h_send.at[a, b], h_recv.at[a, b], at(b, 0, 2 * a)).wait_send()
    for copy in last:
        copy.wait_recv()
    for copy in fins:
        copy.wait_recv()
    best[...] = jnp.max(tops[...], axis=0)[:1]
    for copy in sent + fins:
        copy.wait_send()


def per_device(bin_ids, node_ids, gradients, hessians):
    f32 = jnp.float32
    aux = jnp.stack([node_ids.astype(f32), gradients.astype(f32), hessians.astype(f32)]).reshape(3, ROWS // HALF, HALF)
    dma = pltpu.SemaphoreType.DMA
    table, best = pl.pallas_call(
        kernel,
        out_shape=(
            jax.ShapeDtypeStruct((NX * NY, NODES, BINS), f32),
            jax.ShapeDtypeStruct((1, HALF), f32),
        ),
        in_specs=[pl.BlockSpec(memory_space=pl.ANY)] * 2,
        out_specs=(pl.BlockSpec(memory_space=pltpu.VMEM), pl.BlockSpec(memory_space=pltpu.VMEM)),
        scratch_shapes=[
            pltpu.VMEM((8, NG, ROWS), jnp.int32),
            pltpu.VMEM((8, 3, ROWS // HALF, HALF), f32),
            pltpu.VMEM((8, CH, ROWS), jnp.bfloat16),
            pltpu.VMEM((NG, CH, BINS), f32),
            pltpu.VMEM((4, NZ, QUARTER, BINS), f32),
            pltpu.VMEM((16, 8, HALF), f32),
            dma((2,)),
            dma((8,)), dma((8,)),
            dma((8,)), dma((8,)),
            dma((4, NZ)), dma((4, NZ)),
            dma((NY, NZ)), dma((NY, NZ)),
            dma((NX, NY)), dma((NX, NY)),
            dma((16,)), dma((16,)),
            pltpu.SemaphoreType.REGULAR((2,)),
        ],
        compiler_params=pltpu.CompilerParams(collective_id=0, has_side_effects=True, vmem_limit_bytes=40 * 2**20),
        cost_estimate=pl.CostEstimate(flops=2 * 32 * ROWS * CH * BINS, bytes_accessed=2 * 2**20, transcendentals=0),
        name="split_gains",
    )(bin_ids, aux)
    return table, best[0, :NODES]


def solution(mesh):
    in_specs = (P("feat", "rows"), P("rows"), P("rows"), P("rows"))
    out_specs = (P("feat", None, None), P())
    return jax.shard_map(per_device, mesh=mesh, in_specs=in_specs, out_specs=out_specs, check_vma=False)
```

```python
import functools

import jax
import jax.numpy as jnp
from jax import lax
from jax.experimental import pallas as pl
from jax.experimental.pallas import tpu as pltpu
from jax.sharding import PartitionSpec as P

MESH = pl.DeviceIdType.MESH
BINS = 256
NODES = 32
HALF = 128
NX, NY, NZ = 4, 8, 4
NG = 4
ROWS = 2048
CH = 2 * NODES
QUARTER = 2 * NODES // NZ


def build_weights(aux, weights, slot):
    row = lax.broadcasted_iota(jnp.int32, (CH, HALF), 0)
    node_of = ((row // QUARTER) * 8 + row % 8).astype(jnp.float32)
    is_grad = (row % QUARTER) < 8
    for i in range(ROWS // HALF):
        node = jnp.broadcast_to(aux[slot, 0, i : i + 1, :], (CH, HALF))
        grad = jnp.broadcast_to(aux[slot, 1, i : i + 1, :], (CH, HALF))
        hess = jnp.broadcast_to(aux[slot, 2, i : i + 1, :], (CH, HALF))
        value = jnp.where(node == node_of, jnp.where(is_grad, grad, hess), 0.0)
        weights[slot, :, i * HALF : (i + 1) * HALF] = value.astype(jnp.bfloat16)


def partial_hist(bins, weights, levels, slot, feature):
    ids = bins[slot, pl.ds(feature, 1), :]
    high = jnp.broadcast_to(ids >= HALF, (CH, ROWS))
    low = (ids & (HALF - 1)).astype(jnp.float32).astype(jnp.bfloat16)
    w = weights[slot]
    zero = jnp.zeros_like(w)
    left = jnp.concatenate([jnp.where(high, zero, w), jnp.where(high, w, zero)], axis=0)
    hot = jnp.where(jnp.broadcast_to(low, (HALF, ROWS)) == levels, jnp.bfloat16(1), jnp.bfloat16(0))
    return lax.dot_general(left, hot, (((1,), (1,)), ((), ())), preferred_element_type=jnp.float32)


def side_by_side(d):
    return jnp.concatenate([d[:CH], d[CH:]], axis=1)


def prefix_sums(values):
    r = lax.broadcasted_iota(jnp.int32, (BINS, BINS), 0)
    c = lax.broadcasted_iota(jnp.int32, (BINS, BINS), 1)
    upto = jnp.where(r <= c, 1.0, 0.0).astype(jnp.bfloat16)
    first = values.astype(jnp.bfloat16)
    rest = values - first.astype(jnp.float32)
    second = rest.astype(jnp.bfloat16)
    third = (rest - second.astype(jnp.float32)).astype(jnp.bfloat16)
    n = values.shape[0]
    parts = jnp.concatenate([first.astype(jnp.float32), second.astype(jnp.float32), third.astype(jnp.float32)], axis=0)
    sums = jnp.dot(parts.astype(jnp.bfloat16), upto, preferred_element_type=jnp.float32)
    left = (sums[2 * n :] + sums[n : 2 * n]) + sums[:n]
    total = jnp.broadcast_to(left[:, BINS - 1 :], left.shape)
    return left, total


def kernel(bins_hbm, aux_hbm, table, best,
           bins, aux, weights, acc, inbox, tops, tops_z, tops_y,
           local_sems, a_send, a_recv, w_send, w_recv, h_send, h_recv,
           g_send, g_recv, x_send, x_recv, f_send, f_recv, fz_send, fz_recv, fy_send, fy_recv, ready):
    r = lax.axis_index("rows")
    f = lax.axis_index("feat")
    zh, x, y = r // (NX * NY), (r // NY) % NX, r % NY
    zl, core = f // 2, f % 2
    yh, yl = y // 2, y % 2

    def at(dz, dx, dy, dzl=0, dc=0):
        row = (((zh + dz) % NZ) * NX + (x + dx) % NX) * NY + (y + dy) % NY
        return (row, ((zl + dzl) % 2) * 2 + (core + dc) % 2)

    def pair(dx, p):
        return at(0, dx, (1 - 2 * yl) * p)

    def remote(src, dst, send, recv, to):
        return pltpu.make_async_remote_copy(src_ref=src, dst_ref=dst, send_sem=send, recv_sem=recv, device_id=to, device_id_type=MESH)

    barrier = pltpu.get_barrier_semaphore()
    near = [pair(2, 1), pair(1, 1), pair(3, 1), at(0, 2, 0), at(0, 1, 0), at(0, 3, 0),
            at(0, 0, 2), at(0, 0, 6), at(1, 0, 0), at(3, 0, 0), at(0, 0, 1), at(0, 0, 7),
            at(0, 0, 0, 1, 0), at(0, 0, 0, 0, 1), at(0, 0, 0, 1, 1)]
    for to in near:
        pl.semaphore_signal(barrier, inc=1, device_id=to, device_id_type=MESH)

    def features_of(dx, p):
        group = ((x + dx) % NX) * 2 + (yl + p) % 2
        return pl.ds(group * NG, NG)

    own_bins = pltpu.make_async_copy(bins_hbm.at[features_of(0, 0)], bins.at[0], local_sems.at[0])
    own_aux = pltpu.make_async_copy(aux_hbm, aux.at[0], local_sems.at[1])
    own_bins.start()
    own_aux.start()
    pl.semaphore_wait(barrier, len(near))

    exchange = {}
    for dx, p in ((1, 0), (3, 0), (0, 1), (2, 0), (1, 1), (3, 1), (2, 1)):
        s = dx * 2 + p
        to = pair(dx, p)
        exchange[s] = (
            remote(aux_hbm, aux.at[s], w_send.at[s], w_recv.at[s], to),
            remote(bins_hbm.at[features_of(dx, p)], bins.at[s], a_send.at[s], a_recv.at[s], to),
        )
        for copy in exchange[s]:
            copy.start()
    for to in (at(0, 0, 2), at(0, 0, 6), at(1, 0, 0), at(3, 0, 0)):
        pl.semaphore_signal(ready.at[0], inc=1, device_id=to, device_id_type=MESH)

    levels = lax.broadcasted_iota(jnp.int32, (HALF, ROWS), 0).astype(jnp.float32).astype(jnp.bfloat16)
    own_aux.wait()
    own_bins.wait()
    build_weights(aux, weights, 0)

    @pl.loop(0, NG, unroll=4)
    def _(j):
        acc[j] = side_by_side(partial_hist(bins, weights, levels, 0, j))

    pl.semaphore_wait(ready.at[0], 4)
    for d in (2, 1, 3):
        pl.semaphore_signal(ready.at[1], inc=1, device_id=at(d, 0, 0), device_id_type=MESH)

    for s in (2, 6, 1, 4, 3, 7):
        for copy in exchange[s]:
            copy.wait()
        build_weights(aux, weights, s)

        @pl.loop(0, NG, unroll=4)
        def _(j):
            acc[j] = acc[j] + side_by_side(partial_hist(bins, weights, levels, s, j))

    for copy in exchange[5]:
        copy.wait()
    build_weights(aux, weights, 5)
    pl.semaphore_wait(ready.at[1], 3)

    @pl.loop(0, NG, unroll=4)
    def _(i):
        m = (i + 1) // 2
        a = (2 + m * (1 - 2 * (i % 2))) % 4
        j = (yh + a) % 4
        acc[j] = acc[j] + side_by_side(partial_hist(bins, weights, levels, 5, j))
        for b in (2, 1, 3, 0):
            quarter = pl.ds(pl.multiple_of(((zh + b) % NZ) * QUARTER, QUARTER), QUARTER)

            @pl.when(a + b > 0)
            def _():
                remote(acc.at[j, quarter], inbox.at[a, b], h_send.at[a, b], h_recv.at[a, b], at(b, 0, 2 * a)).start()

    hist = acc[yh, pl.ds(pl.multiple_of(zh * QUARTER, QUARTER), QUARTER), :]
    others = [(a, b) for a in (0, 1, 3, 2) for b in (0, 1, 3, 2) if a or b]
    for a, b in others:
        remote(acc.at[0, pl.ds(0, QUARTER)], inbox.at[a, b], h_send.at[a, b], h_recv.at[a, b], at(b, 0, 2 * a)).wait_recv()
        hist = hist + inbox[a, b]

    left, whole = prefix_sums(hist)
    lg, lh, tg, th = left[:8], left[8:], whole[:8], whole[8:]
    rg, rh = tg - lg, th - lh
    gains = lg * lg / (lh + 1.0) + rg * rg / (rh + 1.0) - tg * tg / (th + 1.0)

    def feature_at(dy):
        there = (y + dy) % NY
        return (x * 2 + there % 2) * NG + there // 2

    me = feature_at(0)
    rows = pl.ds(pl.multiple_of(zh * 8, 8), 8)
    table[me, rows, :] = gains

    def gain_rows(dy, dz):
        return table.at[feature_at(NY - dy), pl.ds(pl.multiple_of(((zh + NZ - dz) % NZ) * 8, 8), 8)]

    offsets = sorted(((dy, dz) for dy in range(NY) for dz in range(NZ)), key=lambda o: min(o[0], NY - o[0]) + 2 * min(o[1], NZ - o[1]))
    sent = []
    arrive = {}
    last = []

    def forward(dy, dz):
        for dx in (1, 3, 2):
            copy = remote(gain_rows(dy, dz), gain_rows(dy, dz), x_send.at[dx, dy, dz], x_recv.at[dx, dy, dz], at(0, dx, 0))
            copy.start()
            sent.append(copy)
            last.append(copy)

    for dy, dz in offsets[1:]:
        copy = remote(gain_rows(0, 0), gain_rows(0, 0), g_send.at[dy, dz], g_recv.at[dy, dz], at(dz, 0, dy))
        copy.start()
        sent.append(copy)
        arrive[dy, dz] = copy

    lane = lax.broadcasted_iota(jnp.int32, (8, HALF), 1)
    node = lax.broadcasted_iota(jnp.int32, (8, HALF), 0) + zh * 8
    top = jnp.broadcast_to(jnp.max(gains, axis=1, keepdims=True), (8, HALF))
    top = jnp.max(jnp.where(lane == node, top, -jnp.inf), axis=0, keepdims=True)

    def share(top, slots, send, recv, partners):
        slots[0] = jnp.broadcast_to(top, (8, HALF))
        copies = []
        for n, to in enumerate(partners, 1):
            copies.append(remote(slots.at[0], slots.at[n], send.at[n], recv.at[n], to))
            copies[-1].start()
        sent.extend(copies)
        return copies

    def gather_top(slots, copies):
        for copy in copies:
            copy.wait_recv()
        return jnp.max(slots[...], axis=0)[:1]

    shared = share(top, tops, f_send, f_recv, [at(0, n // 4, 0, (n // 2) % 2, n % 2) for n in range(1, 16)])
    forward(0, 0)
    for n, (dy, dz) in enumerate(offsets[1:]):
        arrive[dy, dz].wait_recv()
        forward(dy, dz)
        if n == 9:
            shared = share(gather_top(tops, shared), tops_z, fz_send, fz_recv, [at(d, 0, 0) for d in (1, 3, 2)])
        if n == 21:
            shared = share(gather_top(tops_z, shared), tops_y, fy_send, fy_recv, [at(0, 0, d) for d in (4, 3, 5, 2, 6, 1, 7)])

    for a, b in others:
        remote(acc.at[0, pl.ds(0, QUARTER)], inbox.at[a, b], h_send.at[a, b], h_recv.at[a, b], at(b, 0, 2 * a)).wait_send()
    for copy in last:
        copy.wait_recv()
    best[...] = gather_top(tops_y, shared)
    for copy in sent:
        copy.wait_send()


def per_device(bin_ids, node_ids, gradients, hessians):
    f32 = jnp.float32
    aux = jnp.stack([node_ids.astype(f32), gradients.astype(f32), hessians.astype(f32)]).reshape(3, ROWS // HALF, HALF)
    dma = pltpu.SemaphoreType.DMA
    table, best = pl.pallas_call(
        kernel,
        out_shape=(
            jax.ShapeDtypeStruct((NX * NY, NODES, BINS), f32),
            jax.ShapeDtypeStruct((1, HALF), f32),
        ),
        in_specs=[pl.BlockSpec(memory_space=pl.ANY)] * 2,
        out_specs=(pl.BlockSpec(memory_space=pltpu.VMEM), pl.BlockSpec(memory_space=pltpu.VMEM)),
        scratch_shapes=[
            pltpu.VMEM((8, NG, ROWS), jnp.int32),
            pltpu.VMEM((8, 3, ROWS // HALF, HALF), f32),
            pltpu.VMEM((8, CH, ROWS), jnp.bfloat16),
            pltpu.VMEM((NG, CH, BINS), f32),
            pltpu.VMEM((4, NZ, QUARTER, BINS), f32),
            pltpu.VMEM((16, 8, HALF), f32),
            pltpu.VMEM((NZ, 8, HALF), f32),
            pltpu.VMEM((NY, 8, HALF), f32),
            dma((2,)),
            dma((8,)), dma((8,)),
            dma((8,)), dma((8,)),
            dma((4, NZ)), dma((4, NZ)),
            dma((NY, NZ)), dma((NY, NZ)),
            dma((NX, NY, NZ)), dma((NX, NY, NZ)),
            dma((16,)), dma((16,)),
            dma((NZ,)), dma((NZ,)),
            dma((NY,)), dma((NY,)),
            pltpu.SemaphoreType.REGULAR((2,)),
        ],
        compiler_params=pltpu.CompilerParams(collective_id=0, has_side_effects=True, vmem_limit_bytes=40 * 2**20),
        cost_estimate=pl.CostEstimate(flops=2 * 32 * ROWS * CH * BINS, bytes_accessed=2 * 2**20, transcendentals=0),
        name="split_gains",
    )(bin_ids, aux)
    return table, best[0, :NODES]


def solution(mesh):
    in_specs = (P("feat", "rows"), P("rows"), P("rows"), P("rows"))
    out_specs = (P("feat", None, None), P())
    return jax.shard_map(per_device, mesh=mesh, in_specs=in_specs, out_specs=out_specs, check_vma=False)
```

```python
import functools

import jax
import jax.numpy as jnp
from jax import lax
from jax.experimental import pallas as pl
from jax.experimental.pallas import tpu as pltpu
from jax.sharding import PartitionSpec as P

MESH = pl.DeviceIdType.MESH
BINS = 256
NODES = 32
HALF = 128
NX, NY, NZ = 4, 8, 4
NG = 4
ROWS = 2048
CH = 2 * NODES
QUARTER = 2 * NODES // NZ


def build_weights(aux, weights, slot):
    row = lax.broadcasted_iota(jnp.int32, (CH, HALF), 0)
    node_of = ((row // QUARTER) * 8 + row % 8).astype(jnp.float32)
    is_grad = (row % QUARTER) < 8
    for i in range(ROWS // HALF):
        node = jnp.broadcast_to(aux[slot, 0, i : i + 1, :], (CH, HALF))
        grad = jnp.broadcast_to(aux[slot, 1, i : i + 1, :], (CH, HALF))
        hess = jnp.broadcast_to(aux[slot, 2, i : i + 1, :], (CH, HALF))
        value = jnp.where(node == node_of, jnp.where(is_grad, grad, hess), 0.0)
        weights[slot, :, i * HALF : (i + 1) * HALF] = value.astype(jnp.bfloat16)


def partial_hist(bins, weights, levels, slot, feature):
    ids = bins[slot, pl.ds(feature, 1), :]
    high = jnp.broadcast_to(ids >= HALF, (CH, ROWS))
    low = (ids & (HALF - 1)).astype(jnp.float32).astype(jnp.bfloat16)
    w = weights[slot]
    zero = jnp.zeros_like(w)
    left = jnp.concatenate([jnp.where(high, zero, w), jnp.where(high, w, zero)], axis=0)
    hot = jnp.where(jnp.broadcast_to(low, (HALF, ROWS)) == levels, jnp.bfloat16(1), jnp.bfloat16(0))
    return lax.dot_general(left, hot, (((1,), (1,)), ((), ())), preferred_element_type=jnp.float32)


def side_by_side(d):
    return jnp.concatenate([d[:CH], d[CH:]], axis=1)


def prefix_sums(values):
    r = lax.broadcasted_iota(jnp.int32, (BINS, BINS), 0)
    c = lax.broadcasted_iota(jnp.int32, (BINS, BINS), 1)
    upto = jnp.where(r <= c, 1.0, 0.0).astype(jnp.bfloat16)
    first = values.astype(jnp.bfloat16)
    rest = values - first.astype(jnp.float32)
    second = rest.astype(jnp.bfloat16)
    third = (rest - second.astype(jnp.float32)).astype(jnp.bfloat16)
    n = values.shape[0]
    parts = jnp.concatenate([first.astype(jnp.float32), second.astype(jnp.float32), third.astype(jnp.float32)], axis=0)
    sums = jnp.dot(parts.astype(jnp.bfloat16), upto, preferred_element_type=jnp.float32)
    left = (sums[2 * n :] + sums[n : 2 * n]) + sums[:n]
    total = jnp.broadcast_to(left[:, BINS - 1 :], left.shape)
    return left, total


def kernel(bins_hbm, aux_hbm, table, best,
           bins, aux, weights, acc, inbox, tops, tops_z, tops_y,
           local_sems, a_send, a_recv, w_send, w_recv, h_send, h_recv,
           g_send, g_recv, x_send, x_recv, f_send, f_recv, ready):
    r = lax.axis_index("rows")
    f = lax.axis_index("feat")
    zh, x, y = r // (NX * NY), (r // NY) % NX, r % NY
    zl, core = f // 2, f % 2
    yh, yl = y // 2, y % 2

    def at(dz, dx, dy, dzl=0, dc=0):
        row = (((zh + dz) % NZ) * NX + (x + dx) % NX) * NY + (y + dy) % NY
        return (row, ((zl + dzl) % 2) * 2 + (core + dc) % 2)

    def pair(dx, p):
        return at(0, dx, (1 - 2 * yl) * p)

    def remote(src, dst, send, recv, to):
        return pltpu.make_async_remote_copy(src_ref=src, dst_ref=dst, send_sem=send, recv_sem=recv, device_id=to, device_id_type=MESH)

    barrier = pltpu.get_barrier_semaphore()
    near = [pair(2, 1), pair(1, 1), pair(3, 1), at(0, 2, 0), at(0, 1, 0), at(0, 3, 0),
            at(0, 0, 2), at(0, 0, 6), at(1, 0, 0), at(3, 0, 0), at(0, 0, 1), at(0, 0, 7),
            at(0, 0, 0, 1, 0), at(0, 0, 0, 0, 1), at(0, 0, 0, 1, 1)]
    for to in near:
        pl.semaphore_signal(barrier, inc=1, device_id=to, device_id_type=MESH)

    def features_of(dx, p):
        group = ((x + dx) % NX) * 2 + (yl + p) % 2
        return pl.ds(group * NG, NG)

    own_bins = pltpu.make_async_copy(bins_hbm.at[features_of(0, 0)], bins.at[0], local_sems.at[0])
    own_aux = pltpu.make_async_copy(aux_hbm, aux.at[0], local_sems.at[1])
    own_bins.start()
    own_aux.start()
    pl.semaphore_wait(barrier, len(near))

    exchange = {}
    for dx, p in ((1, 0), (3, 0), (0, 1), (2, 0), (1, 1), (3, 1), (2, 1)):
        s = dx * 2 + p
        to = pair(dx, p)
        exchange[s] = (
            remote(aux_hbm, aux.at[s], w_send.at[0], w_recv.at[s], to),
            remote(bins_hbm.at[features_of(dx, p)], bins.at[s], a_send.at[0], a_recv.at[s], to),
        )
        for copy in exchange[s]:
            copy.start()
    for to in (at(0, 0, 2), at(0, 0, 6), at(1, 0, 0), at(3, 0, 0)):
        pl.semaphore_signal(ready.at[0], inc=1, device_id=to, device_id_type=MESH)

    levels = lax.broadcasted_iota(jnp.int32, (HALF, ROWS), 0).astype(jnp.float32).astype(jnp.bfloat16)
    own_aux.wait()
    own_bins.wait()
    build_weights(aux, weights, 0)

    @pl.loop(0, NG, unroll=4)
    def _(j):
        acc[j] = side_by_side(partial_hist(bins, weights, levels, 0, j))

    pl.semaphore_wait(ready.at[0], 4)
    for d in (2, 1, 3):
        pl.semaphore_signal(ready.at[1], inc=1, device_id=at(d, 0, 0), device_id_type=MESH)

    for s in (2, 6, 1, 4, 3, 7):
        for copy in exchange[s]:
            copy.wait_recv()
        build_weights(aux, weights, s)

        @pl.loop(0, NG, unroll=4)
        def _(j):
            acc[j] = acc[j] + side_by_side(partial_hist(bins, weights, levels, s, j))

    for copy in exchange[5]:
        copy.wait_recv()
    build_weights(aux, weights, 5)
    pl.semaphore_wait(ready.at[1], 3)

    @pl.loop(0, NG, unroll=4)
    def _(i):
        m = (i + 1) // 2
        a = (2 + m * (1 - 2 * (i % 2))) % 4
        j = (yh + a) % 4
        acc[j] = acc[j] + side_by_side(partial_hist(bins, weights, levels, 5, j))
        for b in (2, 1, 3, 0):
            quarter = pl.ds(pl.multiple_of(((zh + b) % NZ) * QUARTER, QUARTER), QUARTER)

            @pl.when(a + b > 0)
            def _():
                remote(acc.at[j, quarter], inbox.at[a, b], h_send.at[(a + 3) // 4], h_recv.at[(a + 3) // 4], at(b, 0, 2 * a)).start()

    hist = acc[yh, pl.ds(pl.multiple_of(zh * QUARTER, QUARTER), QUARTER), :]
    nearby = remote(inbox.at[0, pl.ds(1, 3)], inbox.at[0, pl.ds(1, 3)], h_send.at[0], h_recv.at[0], at(1, 0, 0))
    beyond = remote(inbox.at[pl.ds(1, 3)], inbox.at[pl.ds(1, 3)], h_send.at[1], h_recv.at[1], at(1, 0, 0))
    nearby.wait_recv()
    for b in range(1, 4):
        hist = hist + inbox[0, b]
    beyond.wait_recv()
    for a in range(1, 4):
        hist = hist + ((inbox[a, 0] + inbox[a, 1]) + (inbox[a, 2] + inbox[a, 3]))

    left, whole = prefix_sums(hist)
    lg, lh, tg, th = left[:8], left[8:], whole[:8], whole[8:]
    rg, rh = tg - lg, th - lh
    gains = lg * lg / (lh + 1.0) + rg * rg / (rh + 1.0) - tg * tg / (th + 1.0)

    def feature_at(dy):
        there = (y + dy) % NY
        return (x * 2 + there % 2) * NG + there // 2

    me = feature_at(0)
    rows = pl.ds(pl.multiple_of(zh * 8, 8), 8)
    table[me, rows, :] = gains

    def gain_rows(dy, dz):
        return table.at[feature_at(NY - dy), pl.ds(pl.multiple_of(((zh + NZ - dz) % NZ) * 8, 8), 8)]

    offsets = sorted(((dy, dz) for dy in range(NY) for dz in range(NZ)), key=lambda o: min(o[0], NY - o[0]) + 2 * min(o[1], NZ - o[1]))
    arrive = {}

    def forward(dy, dz):
        for dx in (1, 3, 2):
            remote(gain_rows(dy, dz), gain_rows(dy, dz), x_send, x_recv, at(0, dx, 0)).start()

    for dy, dz in offsets[1:]:
        arrive[dy, dz] = remote(gain_rows(0, 0), gain_rows(0, 0), g_send.at[min(dy, 1)], g_recv.at[dy, dz], at(dz, 0, dy))
        arrive[dy, dz].start()

    lane = lax.broadcasted_iota(jnp.int32, (8, HALF), 1)
    node = lax.broadcasted_iota(jnp.int32, (8, HALF), 0) + zh * 8
    top = jnp.broadcast_to(jnp.max(gains, axis=1, keepdims=True), (8, HALF))
    top = jnp.max(jnp.where(lane == node, top, -jnp.inf), axis=0, keepdims=True)

    def share(top, slots, n, partners):
        slots[0] = jnp.broadcast_to(top, (8, HALF))
        for m, to in enumerate(partners, 1):
            remote(slots.at[0], slots.at[m], f_send.at[n], f_recv.at[n], to).start()

    def shared(slots, n):
        others = slots.at[pl.ds(1, slots.shape[0] - 1)]
        return remote(others, others, f_send.at[n], f_recv.at[n], at(1, 0, 0))

    def gather_top(slots, n):
        shared(slots, n).wait_recv()
        return jnp.max(slots[...], axis=0)[:1]

    share(top, tops, 0, [at(0, n // 4, 0, (n // 2) % 2, n % 2) for n in range(1, 16)])
    forward(0, 0)
    for n, (dy, dz) in enumerate(offsets[1:]):
        arrive[dy, dz].wait_recv()
        forward(dy, dz)
        if n == 9:
            share(gather_top(tops, 0), tops_z, 1, [at(d, 0, 0) for d in (1, 3, 2)])
        if n == 21:
            share(gather_top(tops_z, 1), tops_y, 2, [at(0, 0, d) for d in (4, 3, 5, 2, 6, 1, 7)])

    planes = table.at[pl.ds(0, 3 * NY)]
    passed_on = remote(planes, planes, x_send, x_recv, at(0, 1, 0))
    passed_on.wait_recv()
    best[...] = gather_top(tops_y, 2)[:, :NODES]

    passed_on.wait_send()
    along_z = table.at[0, pl.ds(0, 8 * (NZ - 1))]
    along_y = table.at[pl.ds(0, NY - 1)]
    remote(along_z, along_z, g_send.at[0], x_recv, at(1, 0, 0)).wait_send()
    remote(along_y, along_y, g_send.at[1], x_recv, at(0, 0, 1)).wait_send()
    for n, slots in enumerate((tops, tops_z, tops_y)):
        shared(slots, n).wait_send()
    nearby.wait_send()
    beyond.wait_send()
    remote(aux.at[pl.ds(1, 7)], aux.at[pl.ds(1, 7)], w_send.at[0], w_recv.at[1], at(1, 0, 0)).wait_send()
    remote(bins.at[pl.ds(1, 7)], bins.at[pl.ds(1, 7)], a_send.at[0], a_recv.at[1], at(1, 0, 0)).wait_send()


def per_device(bin_ids, node_ids, gradients, hessians):
    f32 = jnp.float32
    aux = jnp.stack([node_ids.astype(f32), gradients.astype(f32), hessians.astype(f32)]).reshape(3, ROWS // HALF, HALF)
    dma = pltpu.SemaphoreType.DMA
    table, best = pl.pallas_call(
        kernel,
        out_shape=(
            jax.ShapeDtypeStruct((NX * NY, NODES, BINS), f32),
            jax.ShapeDtypeStruct((1, NODES), f32),
        ),
        in_specs=[pl.BlockSpec(memory_space=pl.ANY)] * 2,
        out_specs=(pl.BlockSpec(memory_space=pltpu.VMEM), pl.BlockSpec(memory_space=pltpu.VMEM)),
        scratch_shapes=[
            pltpu.VMEM((8, NG, ROWS), jnp.int32),
            pltpu.VMEM((8, 3, ROWS // HALF, HALF), f32),
            pltpu.VMEM((8, CH, ROWS), jnp.bfloat16),
            pltpu.VMEM((NG, CH, BINS), f32),
            pltpu.VMEM((4, NZ, QUARTER, BINS), f32),
            pltpu.VMEM((16, 8, HALF), f32),
            pltpu.VMEM((NZ, 8, HALF), f32),
            pltpu.VMEM((NY, 8, HALF), f32),
            dma((2,)),
            dma((1,)), dma((8,)),
            dma((1,)), dma((8,)),
            dma((2,)), dma((2,)),
            dma((2,)), dma((NY, NZ)),
            dma, dma,
            dma((3,)), dma((3,)),
            pltpu.SemaphoreType.REGULAR((2,)),
        ],
        compiler_params=pltpu.CompilerParams(collective_id=0, has_side_effects=True, vmem_limit_bytes=40 * 2**20),
        cost_estimate=pl.CostEstimate(flops=2 * 32 * ROWS * CH * BINS, bytes_accessed=2 * 2**20, transcendentals=0),
        name="split_gains",
    )(bin_ids, aux)
    return table, best.reshape(NODES)


def solution(mesh):
    in_specs = (P("feat", "rows"), P("rows"), P("rows"), P("rows"))
    out_specs = (P("feat", None, None), P())
    return jax.shard_map(per_device, mesh=mesh, in_specs=in_specs, out_specs=out_specs, check_vma=False)
```

```python
import functools

import jax
import jax.numpy as jnp
from jax import lax
from jax.experimental import pallas as pl
from jax.experimental.pallas import tpu as pltpu
from jax.sharding import PartitionSpec as P

MESH = pl.DeviceIdType.MESH
BINS = 256
NODES = 32
HALF = 128
NX, NY, NZ = 4, 8, 4
NG = 4
ROWS = 2048
CH = 2 * NODES
QUARTER = 2 * NODES // NZ


def build_weights(aux, weights, slot):
    row = lax.broadcasted_iota(jnp.int32, (CH, HALF), 0)
    node_of = ((row // QUARTER) * 8 + row % 8).astype(jnp.float32)
    is_grad = (row % QUARTER) < 8
    for i in range(ROWS // HALF):
        node = jnp.broadcast_to(aux[slot, 0, i : i + 1, :], (CH, HALF))
        grad = jnp.broadcast_to(aux[slot, 1, i : i + 1, :], (CH, HALF))
        hess = jnp.broadcast_to(aux[slot, 2, i : i + 1, :], (CH, HALF))
        value = jnp.where(node == node_of, jnp.where(is_grad, grad, hess), 0.0)
        weights[slot, :, i * HALF : (i + 1) * HALF] = value.astype(jnp.bfloat16)


def partial_hist(bins, weights, levels, slot, feature):
    ids = bins[slot, pl.ds(feature, 1), :]
    high = jnp.broadcast_to(ids >= HALF, (CH, ROWS))
    low = (ids & (HALF - 1)).astype(jnp.float32).astype(jnp.bfloat16)
    w = weights[slot]
    zero = jnp.zeros_like(w)
    left = jnp.concatenate([jnp.where(high, zero, w), jnp.where(high, w, zero)], axis=0)
    hot = jnp.where(jnp.broadcast_to(low, (HALF, ROWS)) == levels, jnp.bfloat16(1), jnp.bfloat16(0))
    return lax.dot_general(left, hot, (((1,), (1,)), ((), ())), preferred_element_type=jnp.float32)


def side_by_side(d):
    return jnp.concatenate([d[:CH], d[CH:]], axis=1)


def prefix_sums(values):
    r = lax.broadcasted_iota(jnp.int32, (BINS, BINS), 0)
    c = lax.broadcasted_iota(jnp.int32, (BINS, BINS), 1)
    upto = jnp.where(r <= c, 1.0, 0.0).astype(jnp.bfloat16)
    first = values.astype(jnp.bfloat16)
    rest = values - first.astype(jnp.float32)
    second = rest.astype(jnp.bfloat16)
    third = (rest - second.astype(jnp.float32)).astype(jnp.bfloat16)
    n = values.shape[0]
    parts = jnp.concatenate([first.astype(jnp.float32), second.astype(jnp.float32), third.astype(jnp.float32)], axis=0)
    sums = jnp.dot(parts.astype(jnp.bfloat16), upto, preferred_element_type=jnp.float32)
    left = (sums[2 * n :] + sums[n : 2 * n]) + sums[:n]
    total = jnp.broadcast_to(left[:, BINS - 1 :], left.shape)
    return left, total


def kernel(bins_hbm, aux_hbm, table, best,
           bins, aux, weights, acc, inbox, tops, tops_z, tops_y,
           local_sems, a_send, a_recv, w_send, w_recv, h_send, h_recv,
           g_send, g_recv, x_send, x_recv, f_send, f_recv, c_send, c_recv, ready):
    r = lax.axis_index("rows")
    f = lax.axis_index("feat")
    zh, x, y = lax.div(r, NX * NY), lax.rem(lax.div(r, NY), NX), lax.rem(r, NY)
    zl, core = lax.div(f, 2), lax.rem(f, 2)
    yh, yl = lax.div(y, 2), lax.rem(y, 2)
    at_x = [lax.rem(x + d, NX) for d in range(NX)]
    at_y = [lax.rem(y + d, NY) for d in range(NY)]
    at_z = [lax.rem(zh + d, NZ) for d in range(NZ)]

    def at(dz, dx, dy, dzl=0, dc=0):
        there = at_y[dy] if isinstance(dy, int) else lax.rem(y + dy, NY)
        row = (at_z[dz] * NX + at_x[dx]) * NY + there
        return (row, (zl * (1 - dzl) + (1 - zl) * dzl) * 2 + core * (1 - dc) + (1 - core) * dc)

    def pair(dx, p):
        return at(0, dx, (NY + 1 - 2 * yl) * p if p else 0)

    def remote(src, dst, send, recv, to):
        return pltpu.make_async_remote_copy(src_ref=src, dst_ref=dst, send_sem=send, recv_sem=recv, device_id=to, device_id_type=MESH)

    barrier = pltpu.get_barrier_semaphore()
    near = [pair(2, 1), pair(1, 1), pair(3, 1), at(0, 2, 0), at(0, 1, 0), at(0, 3, 0),
            at(0, 0, 2), at(0, 0, 6), at(1, 0, 0), at(3, 0, 0), at(0, 0, 1), at(0, 0, 7),
            at(0, 0, 0, 1, 0), at(0, 0, 0, 0, 1), at(0, 0, 0, 1, 1)]
    for to in near:
        pl.semaphore_signal(barrier, inc=1, device_id=to, device_id_type=MESH)

    def features_of(dx, p):
        group = at_x[dx] * 2 + (yl * (1 - p) + (1 - yl) * p)
        return pl.ds(group * NG, NG)

    own_bins = pltpu.make_async_copy(bins_hbm.at[features_of(0, 0)], bins.at[0], local_sems.at[0])
    own_aux = pltpu.make_async_copy(aux_hbm, aux.at[0], local_sems.at[1])
    own_bins.start()
    own_aux.start()
    pl.semaphore_wait(barrier, len(near))

    exchange = {}
    for dx, p in ((1, 0), (3, 0), (0, 1), (2, 0), (1, 1), (3, 1), (2, 1)):
        s = dx * 2 + p
        to = pair(dx, p)
        exchange[s] = (
            remote(aux_hbm, aux.at[s], w_send.at[0], w_recv.at[s], to),
            remote(bins_hbm.at[features_of(dx, p)], bins.at[s], a_send.at[0], a_recv.at[s], to),
        )
        for copy in exchange[s]:
            copy.start()
    for to in (at(0, 0, 2), at(0, 0, 6), at(1, 0, 0), at(3, 0, 0)):
        pl.semaphore_signal(ready.at[0], inc=1, device_id=to, device_id_type=MESH)

    levels = lax.broadcasted_iota(jnp.int32, (HALF, ROWS), 0).astype(jnp.float32).astype(jnp.bfloat16)
    own_aux.wait()
    own_bins.wait()
    build_weights(aux, weights, 0)

    @pl.loop(0, NG, unroll=4)
    def _(j):
        acc[j] = side_by_side(partial_hist(bins, weights, levels, 0, j))

    pl.semaphore_wait(ready.at[0], 4)
    for d in (2, 1, 3):
        pl.semaphore_signal(ready.at[1], inc=1, device_id=at(d, 0, 0), device_id_type=MESH)

    for s in (2, 6, 1, 4, 3, 7):
        for copy in exchange[s]:
            copy.wait_recv()
        build_weights(aux, weights, s)

        @pl.loop(0, NG, unroll=4)
        def _(j):
            acc[j] = acc[j] + side_by_side(partial_hist(bins, weights, levels, s, j))

    for copy in exchange[5]:
        copy.wait_recv()
    build_weights(aux, weights, 5)
    pl.semaphore_wait(ready.at[1], 3)

    @pl.loop(0, NG, unroll=4)
    def _(i):
        m = (i + 1) // 2
        a = (2 + m * (1 - 2 * (i % 2))) % 4
        j = lax.rem(yh + a, 4)
        acc[j] = acc[j] + side_by_side(partial_hist(bins, weights, levels, 5, j))
        for b in (2, 1, 3, 0):
            quarter = pl.ds(pl.multiple_of(at_z[b] * QUARTER, QUARTER), QUARTER)

            @pl.when(a + b > 0)
            def _():
                remote(acc.at[j, quarter], inbox.at[a, b], h_send.at[(a + 3) // 4], h_recv.at[(a + 3) // 4], at(b, 0, 2 * a)).start()

    hist = acc[yh, pl.ds(pl.multiple_of(zh * QUARTER, QUARTER), QUARTER), :]
    nearby = remote(inbox.at[0, pl.ds(1, 3)], inbox.at[0, pl.ds(1, 3)], h_send.at[0], h_recv.at[0], at(1, 0, 0))
    beyond = remote(inbox.at[pl.ds(1, 3)], inbox.at[pl.ds(1, 3)], h_send.at[1], h_recv.at[1], at(1, 0, 0))
    nearby.wait_recv()
    for b in range(1, 4):
        hist = hist + inbox[0, b]
    beyond.wait_recv()
    for a in range(1, 4):
        hist = hist + ((inbox[a, 0] + inbox[a, 1]) + (inbox[a, 2] + inbox[a, 3]))

    left, whole = prefix_sums(hist)
    lg, lh, tg, th = left[:8], left[8:], whole[:8], whole[8:]
    rg, rh = tg - lg, th - lh
    gains = lg * lg / (lh + 1.0) + rg * rg / (rh + 1.0) - tg * tg / (th + 1.0)

    def feature_at(dy):
        there = at_y[dy % NY]
        return (x * 2 + lax.rem(there, 2)) * NG + lax.div(there, 2)

    me = feature_at(0)
    rows = pl.ds(pl.multiple_of(zh * 8, 8), 8)
    table[me, rows, :] = gains

    def gain_rows(dy, dz):
        return table.at[feature_at(NY - dy), pl.ds(pl.multiple_of(at_z[(NZ - dz) % NZ] * 8, 8), 8)]

    offsets = sorted(((dy, dz) for dy in range(NY) for dz in range(NZ)), key=lambda o: min(o[0], NY - o[0]) + 2 * min(o[1], NZ - o[1]))
    arrive = {}

    def forward(dy, dz):
        for dx in (1, 3):
            remote(gain_rows(dy, dz), gain_rows(dy, dz), x_send, x_recv, at(0, dx, 0)).start()
        first = gain_rows(dy, dz).at[:, pl.ds(0, HALF)]
        remote(first, first, x_send, x_recv, at(0, 2, 0)).start()

    second = table.at[me, rows, pl.ds(HALF, HALF)]
    opposite = table.at[(at_x[2] * 2 + yl) * NG + yh, rows, pl.ds(HALF, HALF)]
    across = remote(second, second, c_send.at[0], c_recv.at[0], at(0, 2, 0))
    across.start()

    for dy, dz in offsets[1:]:
        arrive[dy, dz] = remote(gain_rows(0, 0), gain_rows(0, 0), g_send.at[min(dy, 1)], g_recv.at[dy, dz], at(dz, 0, dy))
        arrive[dy, dz].start()

    lane = lax.broadcasted_iota(jnp.int32, (8, HALF), 1)
    node = lax.broadcasted_iota(jnp.int32, (8, HALF), 0) + zh * 8
    top = jnp.broadcast_to(jnp.max(gains, axis=1, keepdims=True), (8, HALF))
    top = jnp.max(jnp.where(lane == node, top, -jnp.inf), axis=0, keepdims=True)

    def share(top, slots, n, partners):
        slots[0] = jnp.broadcast_to(top, (8, HALF))
        for m, to in enumerate(partners, 1):
            remote(slots.at[0], slots.at[m], f_send.at[n], f_recv.at[n], to).start()

    def shared(slots, n):
        others = slots.at[pl.ds(1, slots.shape[0] - 1)]
        return remote(others, others, f_send.at[n], f_recv.at[n], at(1, 0, 0))

    def gather_top(slots, n):
        shared(slots, n).wait_recv()
        return jnp.max(slots[...], axis=0)[:1]

    share(top, tops, 0, [at(0, n // 4, 0, (n // 2) % 2, n % 2) for n in range(1, 16)])
    forward(0, 0)
    for n, (dy, dz) in enumerate(offsets[1:]):
        arrive[dy, dz].wait_recv()
        forward(dy, dz)
        if n == 10:
            across.wait_recv()
            for to_y, to_z in offsets[1:]:
                remote(opposite, opposite, c_send.at[1], c_recv.at[1], at(to_z, 0, to_y)).start()
        if n == 15:
            share(gather_top(tops, 0), tops_z, 1, [at(d, 0, 0) for d in (1, 3, 2)])
        if n == 27:
            share(gather_top(tops_z, 1), tops_y, 2, [at(0, 0, d) for d in (4, 3, 5, 2, 6, 1, 7)])

    planes = table.at[pl.ds(0, 5 * NY // 2)]
    passed_on = remote(planes, planes, x_send, x_recv, at(0, 1, 0))
    passed_on.wait_recv()
    spread = table.at[pl.ds(0, NY * NZ - 1), pl.ds(0, 8), pl.ds(0, HALF)]
    seconds = remote(spread, spread, c_send.at[1], c_recv.at[1], at(0, 0, 1))
    seconds.wait_recv()
    best[...] = gather_top(tops_y, 2)[:, :NODES]

    passed_on.wait_send()
    across.wait_send()
    seconds.wait_send()
    along_z = table.at[0, pl.ds(0, 8 * (NZ - 1))]
    along_y = table.at[pl.ds(0, NY - 1)]
    remote(along_z, along_z, g_send.at[0], x_recv, at(1, 0, 0)).wait_send()
    remote(along_y, along_y, g_send.at[1], x_recv, at(0, 0, 1)).wait_send()
    for n, slots in enumerate((tops, tops_z, tops_y)):
        shared(slots, n).wait_send()
    nearby.wait_send()
    beyond.wait_send()
    remote(aux.at[pl.ds(1, 7)], aux.at[pl.ds(1, 7)], w_send.at[0], w_recv.at[1], at(1, 0, 0)).wait_send()
    remote(bins.at[pl.ds(1, 7)], bins.at[pl.ds(1, 7)], a_send.at[0], a_recv.at[1], at(1, 0, 0)).wait_send()


def per_device(bin_ids, node_ids, gradients, hessians):
    f32 = jnp.float32
    aux = jnp.stack([node_ids.astype(f32), gradients.astype(f32), hessians.astype(f32)]).reshape(3, ROWS // HALF, HALF)
    dma = pltpu.SemaphoreType.DMA
    table, best = pl.pallas_call(
        kernel,
        out_shape=(
            jax.ShapeDtypeStruct((NX * NY, NODES, BINS), f32),
            jax.ShapeDtypeStruct((1, NODES), f32),
        ),
        in_specs=[pl.BlockSpec(memory_space=pl.ANY)] * 2,
        out_specs=(pl.BlockSpec(memory_space=pltpu.VMEM), pl.BlockSpec(memory_space=pltpu.VMEM)),
        scratch_shapes=[
            pltpu.VMEM((8, NG, ROWS), jnp.int32),
            pltpu.VMEM((8, 3, ROWS // HALF, HALF), f32),
            pltpu.VMEM((8, CH, ROWS), jnp.bfloat16),
            pltpu.VMEM((NG, CH, BINS), f32),
            pltpu.VMEM((4, NZ, QUARTER, BINS), f32),
            pltpu.VMEM((16, 8, HALF), f32),
            pltpu.VMEM((NZ, 8, HALF), f32),
            pltpu.VMEM((NY, 8, HALF), f32),
            dma((2,)),
            dma((1,)), dma((8,)),
            dma((1,)), dma((8,)),
            dma((2,)), dma((2,)),
            dma((2,)), dma((NY, NZ)),
            dma, dma,
            dma((3,)), dma((3,)),
            dma((2,)), dma((2,)),
            pltpu.SemaphoreType.REGULAR((2,)),
        ],
        compiler_params=pltpu.CompilerParams(collective_id=0, has_side_effects=True, vmem_limit_bytes=40 * 2**20),
        cost_estimate=pl.CostEstimate(flops=2 * 32 * ROWS * CH * BINS, bytes_accessed=2 * 2**20, transcendentals=0),
        name="split_gains",
    )(bin_ids, aux)
    return table, best.reshape(NODES)


def solution(mesh):
    in_specs = (P("feat", "rows"), P("rows"), P("rows"), P("rows"))
    out_specs = (P("feat", None, None), P())
    return jax.shard_map(per_device, mesh=mesh, in_specs=in_specs, out_specs=out_specs, check_vma=False)
```

```python
import functools

import jax
import jax.numpy as jnp
from jax import lax
from jax.experimental import pallas as pl
from jax.experimental.pallas import tpu as pltpu
from jax.sharding import PartitionSpec as P

MESH = pl.DeviceIdType.MESH
BINS = 256
NODES = 32
HALF = 128
NX, NY, NZ = 4, 8, 4
NG = 4
ROWS = 2048
CH = 2 * NODES
QUARTER = 2 * NODES // NZ


def build_weights(aux, weights, slot):
    row = lax.broadcasted_iota(jnp.int32, (CH, HALF), 0)
    node_of = ((row // QUARTER) * 8 + row % 8).astype(jnp.float32)
    is_grad = (row % QUARTER) < 8
    for i in range(ROWS // HALF):
        node = jnp.broadcast_to(aux[slot, 0, i : i + 1, :], (CH, HALF))
        grad = jnp.broadcast_to(aux[slot, 1, i : i + 1, :], (CH, HALF))
        hess = jnp.broadcast_to(aux[slot, 2, i : i + 1, :], (CH, HALF))
        value = jnp.where(node == node_of, jnp.where(is_grad, grad, hess), 0.0)
        weights[slot, :, i * HALF : (i + 1) * HALF] = value.astype(jnp.bfloat16)


def partial_hist(bins, weights, levels, slot, feature):
    ids = bins[slot, pl.ds(feature, 1), :]
    high = jnp.broadcast_to(ids >= HALF, (CH, ROWS))
    low = (ids & (HALF - 1)).astype(jnp.float32).astype(jnp.bfloat16)
    w = weights[slot]
    zero = jnp.zeros_like(w)
    left = jnp.concatenate([jnp.where(high, zero, w), jnp.where(high, w, zero)], axis=0)
    hot = jnp.where(jnp.broadcast_to(low, (HALF, ROWS)) == levels, jnp.bfloat16(1), jnp.bfloat16(0))
    return lax.dot_general(left, hot, (((1,), (1,)), ((), ())), preferred_element_type=jnp.float32)


def side_by_side(d):
    return jnp.concatenate([d[:CH], d[CH:]], axis=1)


def prefix_sums(values):
    r = lax.broadcasted_iota(jnp.int32, (BINS, BINS), 0)
    c = lax.broadcasted_iota(jnp.int32, (BINS, BINS), 1)
    upto = jnp.where(r <= c, 1.0, 0.0).astype(jnp.bfloat16)
    first = values.astype(jnp.bfloat16)
    rest = values - first.astype(jnp.float32)
    second = rest.astype(jnp.bfloat16)
    third = (rest - second.astype(jnp.float32)).astype(jnp.bfloat16)
    n = values.shape[0]
    parts = jnp.concatenate([first.astype(jnp.float32), second.astype(jnp.float32), third.astype(jnp.float32)], axis=0)
    sums = jnp.dot(parts.astype(jnp.bfloat16), upto, preferred_element_type=jnp.float32)
    left = (sums[2 * n :] + sums[n : 2 * n]) + sums[:n]
    total = jnp.broadcast_to(left[:, BINS - 1 :], left.shape)
    return left, total


def kernel(bins_hbm, aux_hbm, table, best,
           bins, aux, weights, acc, inbox, tops, tops_z, tops_y,
           local_sems, a_send, a_recv, w_send, w_recv, h_send, h_recv,
           g_send, g_recv, x_send, x_recv, f_send, f_recv, c_send, c_recv, ready):
    r = lax.axis_index("rows")
    f = lax.axis_index("feat")
    zh, x, y = lax.div(r, NX * NY), lax.rem(lax.div(r, NY), NX), lax.rem(r, NY)
    zl, core = lax.div(f, 2), lax.rem(f, 2)
    yh, yl = lax.div(y, 2), lax.rem(y, 2)
    at_x = [lax.rem(x + d, NX) for d in range(NX)]
    at_y = [lax.rem(y + d, NY) for d in range(NY)]
    at_z = [lax.rem(zh + d, NZ) for d in range(NZ)]

    def at(dz, dx, dy, dzl=0, dc=0):
        there = at_y[dy] if isinstance(dy, int) else lax.rem(y + dy, NY)
        row = (at_z[dz] * NX + at_x[dx]) * NY + there
        return (row, (zl * (1 - dzl) + (1 - zl) * dzl) * 2 + core * (1 - dc) + (1 - core) * dc)

    def pair(dx, p):
        return at(0, dx, (NY + 1 - 2 * yl) * p if p else 0)

    def remote(src, dst, send, recv, to):
        return pltpu.make_async_remote_copy(src_ref=src, dst_ref=dst, send_sem=send, recv_sem=recv, device_id=to, device_id_type=MESH)

    barrier = pltpu.get_barrier_semaphore()
    near = [pair(2, 1), pair(1, 1), pair(3, 1), at(0, 2, 0), at(0, 1, 0), at(0, 3, 0),
            at(0, 0, 2), at(0, 0, 6), at(1, 0, 0), at(3, 0, 0), at(0, 0, 1), at(0, 0, 7),
            at(0, 0, 0, 1, 0), at(0, 0, 0, 0, 1), at(0, 0, 0, 1, 1)]
    for to in near:
        pl.semaphore_signal(barrier, inc=1, device_id=to, device_id_type=MESH)

    def features_of(dx, p):
        group = at_x[dx] * 2 + (yl * (1 - p) + (1 - yl) * p)
        return pl.ds(group * NG, NG)

    own_bins = pltpu.make_async_copy(bins_hbm.at[features_of(0, 0)], bins.at[0], local_sems.at[0])
    own_aux = pltpu.make_async_copy(aux_hbm, aux.at[0], local_sems.at[1])
    own_bins.start()
    own_aux.start()
    pl.semaphore_wait(barrier, len(near))

    exchange = {}
    for dx, p in ((1, 0), (3, 0), (0, 1), (2, 0), (1, 1), (3, 1), (2, 1)):
        s = dx * 2 + p
        to = pair(dx, p)
        exchange[s] = (
            remote(aux_hbm, aux.at[s], w_send.at[0], w_recv.at[s], to),
            remote(bins_hbm.at[features_of(dx, p)], bins.at[s], a_send.at[0], a_recv.at[s], to),
        )
        for copy in exchange[s]:
            copy.start()
    for to in (at(0, 0, 2), at(0, 0, 6), at(1, 0, 0), at(3, 0, 0)):
        pl.semaphore_signal(ready.at[0], inc=1, device_id=to, device_id_type=MESH)

    levels = lax.broadcasted_iota(jnp.int32, (HALF, ROWS), 0).astype(jnp.float32).astype(jnp.bfloat16)
    own_aux.wait()
    own_bins.wait()
    build_weights(aux, weights, 0)

    @pl.loop(0, NG, unroll=4)
    def _(j):
        acc[j] = side_by_side(partial_hist(bins, weights, levels, 0, j))

    pl.semaphore_wait(ready.at[0], 4)
    for d in (2, 1, 3):
        pl.semaphore_signal(ready.at[1], inc=1, device_id=at(d, 0, 0), device_id_type=MESH)

    for s in (2, 6, 1, 4, 3, 7):
        for copy in exchange[s]:
            copy.wait_recv()
        build_weights(aux, weights, s)

        @pl.loop(0, NG, unroll=4)
        def _(j):
            acc[j] = acc[j] + side_by_side(partial_hist(bins, weights, levels, s, j))

    for copy in exchange[5]:
        copy.wait_recv()
    build_weights(aux, weights, 5)
    pl.semaphore_wait(ready.at[1], 3)

    @pl.loop(0, NG, unroll=4)
    def _(i):
        m = (i + 1) // 2
        a = (2 + m * (1 - 2 * (i % 2))) % 4
        j = lax.rem(yh + a, 4)
        acc[j] = acc[j] + side_by_side(partial_hist(bins, weights, levels, 5, j))
        for b in (2, 1, 3, 0):
            quarter = pl.ds(pl.multiple_of(at_z[b] * QUARTER, QUARTER), QUARTER)

            @pl.when(a + b > 0)
            def _():
                remote(acc.at[j, quarter], inbox.at[a, b], h_send.at[(a + 3) // 4], h_recv.at[(a + 3) // 4], at(b, 0, 2 * a)).start()

    hist = acc[yh, pl.ds(pl.multiple_of(zh * QUARTER, QUARTER), QUARTER), :]
    nearby = remote(inbox.at[0, pl.ds(1, 3)], inbox.at[0, pl.ds(1, 3)], h_send.at[0], h_recv.at[0], at(1, 0, 0))
    beyond = remote(inbox.at[pl.ds(1, 3)], inbox.at[pl.ds(1, 3)], h_send.at[1], h_recv.at[1], at(1, 0, 0))
    nearby.wait_recv()
    for b in range(1, 4):
        hist = hist + inbox[0, b]
    beyond.wait_recv()
    for a in range(1, 4):
        hist = hist + ((inbox[a, 0] + inbox[a, 1]) + (inbox[a, 2] + inbox[a, 3]))

    left, whole = prefix_sums(hist)
    lg, lh, tg, th = left[:8], left[8:], whole[:8], whole[8:]
    rg, rh = tg - lg, th - lh
    gains = lg * lg / (lh + 1.0) + rg * rg / (rh + 1.0) - tg * tg / (th + 1.0)

    def feature_at(dy):
        there = at_y[dy % NY]
        return (x * 2 + lax.rem(there, 2)) * NG + lax.div(there, 2)

    me = feature_at(0)
    rows = pl.ds(pl.multiple_of(zh * 8, 8), 8)
    table[me, rows, :] = gains

    def gain_rows(dy, dz):
        return table.at[feature_at(NY - dy), pl.ds(pl.multiple_of(at_z[(NZ - dz) % NZ] * 8, 8), 8)]

    offsets = sorted(((dy, dz) for dy in range(NY) for dz in range(NZ)), key=lambda o: min(o[0], NY - o[0]) + 2 * min(o[1], NZ - o[1]))
    arrive = {}

    def forward(dy, dz):
        for dx in (1, 3):
            remote(gain_rows(dy, dz), gain_rows(dy, dz), x_send, x_recv, at(0, dx, 0)).start()
        first = gain_rows(dy, dz).at[:, pl.ds(0, HALF)]
        remote(first, first, x_send, x_recv, at(0, 2, 0)).start()

    second = table.at[me, rows, pl.ds(HALF, HALF)]
    opposite = table.at[(at_x[2] * 2 + yl) * NG + yh, rows, pl.ds(HALF, HALF)]
    across = remote(second, second, c_send.at[0], c_recv.at[0], at(0, 2, 0))
    across.start()

    for dy, dz in offsets[1:]:
        arrive[dy, dz] = remote(gain_rows(0, 0), gain_rows(0, 0), g_send.at[min(dy, 1)], g_recv.at[dy, dz], at(dz, 0, dy))
        arrive[dy, dz].start()

    lane = lax.broadcasted_iota(jnp.int32, (8, HALF), 1)
    node = lax.broadcasted_iota(jnp.int32, (8, HALF), 0) + zh * 8
    top = jnp.broadcast_to(jnp.max(gains, axis=1, keepdims=True), (8, HALF))
    top = jnp.max(jnp.where(lane == node, top, -jnp.inf), axis=0, keepdims=True)

    def share(top, slots, n, partners):
        slots[0] = jnp.broadcast_to(top, (8, HALF))
        for m, to in enumerate(partners, 1):
            remote(slots.at[0], slots.at[m], f_send.at[n], f_recv.at[n], to).start()

    def shared(slots, n):
        others = slots.at[pl.ds(1, slots.shape[0] - 1)]
        return remote(others, others, f_send.at[n], f_recv.at[n], at(1, 0, 0))

    def gather_top(slots, n):
        shared(slots, n).wait_recv()
        return jnp.max(slots[...], axis=0)[:1]

    share(top, tops, 0, [at(0, n // 4, 0, (n // 2) % 2, n % 2) for n in range(1, 16)])
    forward(0, 0)
    for n, (dy, dz) in enumerate(offsets[1:]):
        arrive[dy, dz].wait_recv()
        forward(dy, dz)
        if n == 10:
            across.wait_recv()
            for to_y, to_z in offsets[1:]:
                remote(opposite, opposite, c_send.at[1], c_recv.at[1], at(to_z, 0, to_y)).start()
        if n == 9:
            share(gather_top(tops, 0), tops_z, 1, [at(d, 0, 0) for d in (1, 3, 2)])
        if n == 21:
            share(gather_top(tops_z, 1), tops_y, 2, [at(0, 0, d) for d in (4, 3, 5, 2, 6, 1, 7)])

    planes = table.at[pl.ds(0, 5 * NY // 2)]
    passed_on = remote(planes, planes, x_send, x_recv, at(0, 1, 0))
    passed_on.wait_recv()
    spread = table.at[pl.ds(0, NY * NZ - 1), pl.ds(0, 8), pl.ds(0, HALF)]
    seconds = remote(spread, spread, c_send.at[1], c_recv.at[1], at(0, 0, 1))
    seconds.wait_recv()
    best[...] = gather_top(tops_y, 2)[:, :NODES]

    passed_on.wait_send()
    across.wait_send()
    seconds.wait_send()
    along_z = table.at[0, pl.ds(0, 8 * (NZ - 1))]
    along_y = table.at[pl.ds(0, NY - 1)]
    remote(along_z, along_z, g_send.at[0], x_recv, at(1, 0, 0)).wait_send()
    remote(along_y, along_y, g_send.at[1], x_recv, at(0, 0, 1)).wait_send()
    for n, slots in enumerate((tops, tops_z, tops_y)):
        shared(slots, n).wait_send()
    nearby.wait_send()
    beyond.wait_send()
    remote(aux.at[pl.ds(1, 7)], aux.at[pl.ds(1, 7)], w_send.at[0], w_recv.at[1], at(1, 0, 0)).wait_send()
    remote(bins.at[pl.ds(1, 7)], bins.at[pl.ds(1, 7)], a_send.at[0], a_recv.at[1], at(1, 0, 0)).wait_send()


def per_device(bin_ids, node_ids, gradients, hessians):
    f32 = jnp.float32
    aux = jnp.stack([node_ids.astype(f32), gradients.astype(f32), hessians.astype(f32)]).reshape(3, ROWS // HALF, HALF)
    dma = pltpu.SemaphoreType.DMA
    table, best = pl.pallas_call(
        kernel,
        out_shape=(
            jax.ShapeDtypeStruct((NX * NY, NODES, BINS), f32),
            jax.ShapeDtypeStruct((1, NODES), f32),
        ),
        in_specs=[pl.BlockSpec(memory_space=pl.ANY)] * 2,
        out_specs=(pl.BlockSpec(memory_space=pltpu.VMEM), pl.BlockSpec(memory_space=pltpu.VMEM)),
        scratch_shapes=[
            pltpu.VMEM((8, NG, ROWS), jnp.int32),
            pltpu.VMEM((8, 3, ROWS // HALF, HALF), f32),
            pltpu.VMEM((8, CH, ROWS), jnp.bfloat16),
            pltpu.VMEM((NG, CH, BINS), f32),
            pltpu.VMEM((4, NZ, QUARTER, BINS), f32),
            pltpu.VMEM((16, 8, HALF), f32),
            pltpu.VMEM((NZ, 8, HALF), f32),
            pltpu.VMEM((NY, 8, HALF), f32),
            dma((2,)),
            dma((1,)), dma((8,)),
            dma((1,)), dma((8,)),
            dma((2,)), dma((2,)),
            dma((2,)), dma((NY, NZ)),
            dma, dma,
            dma((3,)), dma((3,)),
            dma((2,)), dma((2,)),
            pltpu.SemaphoreType.REGULAR((2,)),
        ],
        compiler_params=pltpu.CompilerParams(collective_id=0, has_side_effects=True, vmem_limit_bytes=40 * 2**20),
        cost_estimate=pl.CostEstimate(flops=2 * 32 * ROWS * CH * BINS, bytes_accessed=2 * 2**20, transcendentals=0),
        name="split_gains",
    )(bin_ids, aux)
    return table, best.reshape(NODES)


def solution(mesh):
    in_specs = (P("feat", "rows"), P("rows"), P("rows"), P("rows"))
    out_specs = (P("feat", None, None), P())
    return jax.shard_map(per_device, mesh=mesh, in_specs=in_specs, out_specs=out_specs, check_vma=False)
```

```python
import functools

import jax
import jax.numpy as jnp
from jax import lax
from jax.experimental import pallas as pl
from jax.experimental.pallas import tpu as pltpu
from jax.sharding import PartitionSpec as P

MESH = pl.DeviceIdType.MESH
BINS = 256
NODES = 32
HALF = 128
NX, NY, NZ = 4, 8, 4
NG = 4
ROWS = 2048
CH = 2 * NODES
QUARTER = 2 * NODES // NZ


def build_weights(aux, weights, slot):
    row = lax.broadcasted_iota(jnp.int32, (CH, HALF), 0)
    node_of = ((row // QUARTER) * 8 + row % 8).astype(jnp.float32)
    is_grad = (row % QUARTER) < 8
    for i in range(ROWS // HALF):
        node = jnp.broadcast_to(aux[slot, 0, i : i + 1, :], (CH, HALF))
        grad = jnp.broadcast_to(aux[slot, 1, i : i + 1, :], (CH, HALF))
        hess = jnp.broadcast_to(aux[slot, 2, i : i + 1, :], (CH, HALF))
        value = jnp.where(node == node_of, jnp.where(is_grad, grad, hess), 0.0)
        weights[slot, :, i * HALF : (i + 1) * HALF] = value.astype(jnp.bfloat16)


def partial_hist(bins, weights, levels, slot, feature):
    ids = bins[slot, pl.ds(feature, 1), :]
    high = jnp.broadcast_to(ids >= HALF, (CH, ROWS))
    low = (ids & (HALF - 1)).astype(jnp.float32).astype(jnp.bfloat16)
    w = weights[slot]
    zero = jnp.zeros_like(w)
    left = jnp.concatenate([jnp.where(high, zero, w), jnp.where(high, w, zero)], axis=0)
    hot = jnp.where(jnp.broadcast_to(low, (HALF, ROWS)) == levels, jnp.bfloat16(1), jnp.bfloat16(0))
    return lax.dot_general(left, hot, (((1,), (1,)), ((), ())), preferred_element_type=jnp.float32)


def side_by_side(d):
    return jnp.concatenate([d[:CH], d[CH:]], axis=1)


def prefix_sums(values):
    r = lax.broadcasted_iota(jnp.int32, (BINS, BINS), 0)
    c = lax.broadcasted_iota(jnp.int32, (BINS, BINS), 1)
    upto = jnp.where(r <= c, 1.0, 0.0).astype(jnp.bfloat16)
    first = values.astype(jnp.bfloat16)
    rest = values - first.astype(jnp.float32)
    second = rest.astype(jnp.bfloat16)
    third = (rest - second.astype(jnp.float32)).astype(jnp.bfloat16)
    n = values.shape[0]
    parts = jnp.concatenate([first.astype(jnp.float32), second.astype(jnp.float32), third.astype(jnp.float32)], axis=0)
    sums = jnp.dot(parts.astype(jnp.bfloat16), upto, preferred_element_type=jnp.float32)
    left = (sums[2 * n :] + sums[n : 2 * n]) + sums[:n]
    total = jnp.broadcast_to(left[:, BINS - 1 :], left.shape)
    return left, total


def kernel(bins_hbm, aux_hbm, table, best,
           bins, aux, weights, acc, inbox, tops, tops_z, tops_y,
           local_sems, a_send, a_recv, w_send, w_recv, h_send, h_recv,
           g_send, g_recv, x_send, x_recv, f_send, f_recv, c_send, c_recv, ready):
    r = lax.axis_index("rows")
    f = lax.axis_index("feat")
    zh, x, y = lax.div(r, NX * NY), lax.rem(lax.div(r, NY), NX), lax.rem(r, NY)
    zl, core = lax.div(f, 2), lax.rem(f, 2)
    yh, yl = lax.div(y, 2), lax.rem(y, 2)
    at_x = [lax.rem(x + d, NX) for d in range(NX)]
    at_y = [lax.rem(y + d, NY) for d in range(NY)]
    at_z = [lax.rem(zh + d, NZ) for d in range(NZ)]

    def at(dz, dx, dy, dzl=0, dc=0):
        there = at_y[dy] if isinstance(dy, int) else lax.rem(y + dy, NY)
        row = (at_z[dz] * NX + at_x[dx]) * NY + there
        return (row, (zl * (1 - dzl) + (1 - zl) * dzl) * 2 + core * (1 - dc) + (1 - core) * dc)

    def pair(dx, p):
        return at(0, dx, (NY + 1 - 2 * yl) * p if p else 0)

    def remote(src, dst, send, recv, to):
        return pltpu.make_async_remote_copy(src_ref=src, dst_ref=dst, send_sem=send, recv_sem=recv, device_id=to, device_id_type=MESH)

    barrier = pltpu.get_barrier_semaphore()
    near = [pair(2, 1), pair(1, 1), pair(3, 1), at(0, 2, 0), at(0, 1, 0), at(0, 3, 0),
            at(0, 0, 2), at(0, 0, 6), at(1, 0, 0), at(3, 0, 0), at(0, 0, 1), at(0, 0, 7),
            at(0, 0, 0, 1, 0), at(0, 0, 0, 0, 1), at(0, 0, 0, 1, 1)]
    for to in near:
        pl.semaphore_signal(barrier, inc=1, device_id=to, device_id_type=MESH)

    def features_of(dx, p):
        group = at_x[dx] * 2 + (yl * (1 - p) + (1 - yl) * p)
        return pl.ds(group * NG, NG)

    own_bins = pltpu.make_async_copy(bins_hbm.at[features_of(0, 0)], bins.at[0], local_sems.at[0])
    own_aux = pltpu.make_async_copy(aux_hbm, aux.at[0], local_sems.at[1])
    own_bins.start()
    own_aux.start()
    pl.semaphore_wait(barrier, len(near))

    exchange = {}
    for dx, p in ((1, 0), (3, 0), (0, 1), (2, 0), (1, 1), (3, 1), (2, 1)):
        s = dx * 2 + p
        to = pair(dx, p)
        exchange[s] = (
            remote(aux_hbm, aux.at[s], w_send.at[0], w_recv.at[s], to),
            remote(bins_hbm.at[features_of(dx, p)], bins.at[s], a_send.at[0], a_recv.at[s], to),
        )
        for copy in exchange[s]:
            copy.start()
    for to in (at(0, 0, 2), at(0, 0, 6), at(1, 0, 0), at(3, 0, 0)):
        pl.semaphore_signal(ready.at[0], inc=1, device_id=to, device_id_type=MESH)

    levels = lax.broadcasted_iota(jnp.int32, (HALF, ROWS), 0).astype(jnp.float32).astype(jnp.bfloat16)
    own_aux.wait()
    own_bins.wait()
    build_weights(aux, weights, 0)

    @pl.loop(0, NG, unroll=4)
    def _(j):
        acc[j] = side_by_side(partial_hist(bins, weights, levels, 0, j))

    pl.semaphore_wait(ready.at[0], 4)
    for d in (2, 1, 3):
        pl.semaphore_signal(ready.at[1], inc=1, device_id=at(d, 0, 0), device_id_type=MESH)

    for s in (2, 6, 1, 4, 3, 7):
        for copy in exchange[s]:
            copy.wait_recv()
        build_weights(aux, weights, s)

        @pl.loop(0, NG, unroll=4)
        def _(j):
            acc[j] = acc[j] + side_by_side(partial_hist(bins, weights, levels, s, j))

    for copy in exchange[5]:
        copy.wait_recv()
    build_weights(aux, weights, 5)
    pl.semaphore_wait(ready.at[1], 3)

    @pl.loop(0, NG, unroll=4)
    def _(i):
        m = (i + 1) // 2
        a = (2 + m * (1 - 2 * (i % 2))) % 4
        j = lax.rem(yh + a, 4)
        acc[j] = acc[j] + side_by_side(partial_hist(bins, weights, levels, 5, j))

    for a, b in sorted(((a, b) for a in range(4) for b in range(4) if a or b), key=lambda o: min(o[0], 4 - o[0]) + min(o[1], 4 - o[1])):
        quarter = pl.ds(pl.multiple_of(at_z[b] * QUARTER, QUARTER), QUARTER)
        remote(acc.at[lax.rem(yh + a, 4), quarter], inbox.at[a, b], h_send.at[min(a, 1)], h_recv.at[min(a, 1)], at(b, 0, 2 * a)).start()

    hist = acc[yh, pl.ds(pl.multiple_of(zh * QUARTER, QUARTER), QUARTER), :]
    nearby = remote(inbox.at[0, pl.ds(1, 3)], inbox.at[0, pl.ds(1, 3)], h_send.at[0], h_recv.at[0], at(1, 0, 0))
    beyond = remote(inbox.at[pl.ds(1, 3)], inbox.at[pl.ds(1, 3)], h_send.at[1], h_recv.at[1], at(1, 0, 0))
    nearby.wait_recv()
    for b in range(1, 4):
        hist = hist + inbox[0, b]
    beyond.wait_recv()
    for a in range(1, 4):
        hist = hist + ((inbox[a, 0] + inbox[a, 1]) + (inbox[a, 2] + inbox[a, 3]))

    left, whole = prefix_sums(hist)
    lg, lh, tg, th = left[:8], left[8:], whole[:8], whole[8:]
    rg, rh = tg - lg, th - lh
    gains = lg * lg / (lh + 1.0) + rg * rg / (rh + 1.0) - tg * tg / (th + 1.0)

    def feature_at(dy):
        there = at_y[dy % NY]
        return (x * 2 + lax.rem(there, 2)) * NG + lax.div(there, 2)

    me = feature_at(0)
    rows = pl.ds(pl.multiple_of(zh * 8, 8), 8)
    table[me, rows, :] = gains

    def gain_rows(dy, dz):
        return table.at[feature_at(NY - dy), pl.ds(pl.multiple_of(at_z[(NZ - dz) % NZ] * 8, 8), 8)]

    offsets = sorted(((dy, dz) for dy in range(NY) for dz in range(NZ)), key=lambda o: min(o[0], NY - o[0]) + 2 * min(o[1], NZ - o[1]))
    arrive = {}

    def forward(dy, dz):
        for dx in (1, 3):
            remote(gain_rows(dy, dz), gain_rows(dy, dz), x_send, x_recv, at(0, dx, 0)).start()
        first = gain_rows(dy, dz).at[:, pl.ds(0, HALF)]
        remote(first, first, x_send, x_recv, at(0, 2, 0)).start()

    second = table.at[me, rows, pl.ds(HALF, HALF)]
    opposite = table.at[(at_x[2] * 2 + yl) * NG + yh, rows, pl.ds(HALF, HALF)]
    across = remote(second, second, c_send.at[0], c_recv.at[0], at(0, 2, 0))
    across.start()

    for dy, dz in offsets[1:]:
        arrive[dy, dz] = remote(gain_rows(0, 0), gain_rows(0, 0), g_send.at[min(dy, 1)], g_recv.at[dy, dz], at(dz, 0, dy))
        arrive[dy, dz].start()

    lane = lax.broadcasted_iota(jnp.int32, (8, HALF), 1)
    node = lax.broadcasted_iota(jnp.int32, (8, HALF), 0) + zh * 8
    top = jnp.broadcast_to(jnp.max(gains, axis=1, keepdims=True), (8, HALF))
    top = jnp.max(jnp.where(lane == node, top, -jnp.inf), axis=0, keepdims=True)

    def share(top, slots, n, partners):
        slots[0] = jnp.broadcast_to(top, (8, HALF))
        for m, to in enumerate(partners, 1):
            remote(slots.at[0], slots.at[m], f_send.at[n], f_recv.at[n], to).start()

    def shared(slots, n):
        others = slots.at[pl.ds(1, slots.shape[0] - 1)]
        return remote(others, others, f_send.at[n], f_recv.at[n], at(1, 0, 0))

    def gather_top(slots, n):
        shared(slots, n).wait_recv()
        return jnp.max(slots[...], axis=0)[:1]

    share(top, tops, 0, [at(0, n // 4, 0, (n // 2) % 2, n % 2) for n in range(1, 16)])
    forward(0, 0)
    for n, (dy, dz) in enumerate(offsets[1:]):
        arrive[dy, dz].wait_recv()
        forward(dy, dz)
        if n == 10:
            across.wait_recv()
            for to_y, to_z in offsets[1:]:
                remote(opposite, opposite, c_send.at[1], c_recv.at[1], at(to_z, 0, to_y)).start()
        if n == 9:
            share(gather_top(tops, 0), tops_z, 1, [at(d, 0, 0) for d in (1, 3, 2)])
        if n == 21:
            share(gather_top(tops_z, 1), tops_y, 2, [at(0, 0, d) for d in (4, 3, 5, 2, 6, 1, 7)])

    planes = table.at[pl.ds(0, 5 * NY // 2)]
    passed_on = remote(planes, planes, x_send, x_recv, at(0, 1, 0))
    passed_on.wait_recv()
    spread = table.at[pl.ds(0, NY * NZ - 1), pl.ds(0, 8), pl.ds(0, HALF)]
    seconds = remote(spread, spread, c_send.at[1], c_recv.at[1], at(0, 0, 1))
    seconds.wait_recv()
    best[...] = gather_top(tops_y, 2)[:, :NODES]

    passed_on.wait_send()
    across.wait_send()
    seconds.wait_send()
    along_z = table.at[0, pl.ds(0, 8 * (NZ - 1))]
    along_y = table.at[pl.ds(0, NY - 1)]
    remote(along_z, along_z, g_send.at[0], x_recv, at(1, 0, 0)).wait_send()
    remote(along_y, along_y, g_send.at[1], x_recv, at(0, 0, 1)).wait_send()
    for n, slots in enumerate((tops, tops_z, tops_y)):
        shared(slots, n).wait_send()
    nearby.wait_send()
    beyond.wait_send()
    remote(aux.at[pl.ds(1, 7)], aux.at[pl.ds(1, 7)], w_send.at[0], w_recv.at[1], at(1, 0, 0)).wait_send()
    remote(bins.at[pl.ds(1, 7)], bins.at[pl.ds(1, 7)], a_send.at[0], a_recv.at[1], at(1, 0, 0)).wait_send()


def per_device(bin_ids, node_ids, gradients, hessians):
    f32 = jnp.float32
    aux = jnp.stack([node_ids.astype(f32), gradients.astype(f32), hessians.astype(f32)]).reshape(3, ROWS // HALF, HALF)
    dma = pltpu.SemaphoreType.DMA
    table, best = pl.pallas_call(
        kernel,
        out_shape=(
            jax.ShapeDtypeStruct((NX * NY, NODES, BINS), f32),
            jax.ShapeDtypeStruct((1, NODES), f32),
        ),
        in_specs=[pl.BlockSpec(memory_space=pl.ANY)] * 2,
        out_specs=(pl.BlockSpec(memory_space=pltpu.VMEM), pl.BlockSpec(memory_space=pltpu.VMEM)),
        scratch_shapes=[
            pltpu.VMEM((8, NG, ROWS), jnp.int32),
            pltpu.VMEM((8, 3, ROWS // HALF, HALF), f32),
            pltpu.VMEM((8, CH, ROWS), jnp.bfloat16),
            pltpu.VMEM((NG, CH, BINS), f32),
            pltpu.VMEM((4, NZ, QUARTER, BINS), f32),
            pltpu.VMEM((16, 8, HALF), f32),
            pltpu.VMEM((NZ, 8, HALF), f32),
            pltpu.VMEM((NY, 8, HALF), f32),
            dma((2,)),
            dma((1,)), dma((8,)),
            dma((1,)), dma((8,)),
            dma((2,)), dma((2,)),
            dma((2,)), dma((NY, NZ)),
            dma, dma,
            dma((3,)), dma((3,)),
            dma((2,)), dma((2,)),
            pltpu.SemaphoreType.REGULAR((2,)),
        ],
        compiler_params=pltpu.CompilerParams(collective_id=0, has_side_effects=True, vmem_limit_bytes=40 * 2**20),
        cost_estimate=pl.CostEstimate(flops=2 * 32 * ROWS * CH * BINS, bytes_accessed=2 * 2**20, transcendentals=0),
        name="split_gains",
    )(bin_ids, aux)
    return table, best.reshape(NODES)


def solution(mesh):
    in_specs = (P("feat", "rows"), P("rows"), P("rows"), P("rows"))
    out_specs = (P("feat", None, None), P())
    return jax.shard_map(per_device, mesh=mesh, in_specs=in_specs, out_specs=out_specs, check_vma=False)
```
